512 devices in a mesh: depth: 16 (over x, z_lo), chan: 32 (over y, z_hi, core).
Axes of the slice: x: 4, y: 8, z: 8 (z_hi: 2, z_lo: 4; z = z_hi * 4 + z_lo), core: 2. Of those that a mesh axis runs over, the one named last changes fastest.
Arguments:
- volume: bfloat16 [16, 16, 16, 1024], P('depth', None, None, 'chan'), may hold values from -6 to 6
- cotangent: bfloat16 [16, 16, 16, 1024], P('depth', None, None, 'chan'), may hold values from -6 to 6
- kernel: bfloat16 [1024, 27, 1024], P('chan'), may hold values from -0.0390625 to 0.0390625
Outputs:
- input_grad: bfloat16 [16, 16, 16, 1024], P('depth', None, None, 'chan')
- kernel_grad: float32 [32, 32, 27, 1024], P('chan', None, None, 'depth')
The draws below stay inside these ranges and needn't reach their ends.
All inputs are finite; a program needn't handle non-finite values.
Results may differ from the reference program's by a relative error of at most 0.023.
Values may be sent and summed in bfloat16 or wider, within the bound.
A program may use at most 64 MiB of HBM per device.

```python
import jax
import jax.numpy as jnp
from jax import lax

CH = 1024
DZ = 1
HT = 16
WD = 16
DEP = 16
CS = 32
N_DEPTH = 16
N_CHAN = 32


def block_scale(stream_key, extent, cuts, least, top_value):
    gain = 1.0
    for dim, shards_of in cuts:
        draws = jax.random.uniform(jax.random.fold_in(jax.random.fold_in(stream_key, 6), dim), (shards_of,), jnp.float32, least / len(cuts), top_value / len(cuts))
        gain = gain * jnp.repeat(jnp.exp(draws), extent[dim] // shards_of).reshape((-1,) + (1,) * (len(extent) - 1 - dim))
    return gain


def normal_values(own_key, shape, scale, most, pieces=(), held_as=jnp.bfloat16):
    gain = block_scale(own_key, shape, pieces, -0.22, 0.18) if pieces else 1.0
    result = jax.random.normal(own_key, shape, jnp.float32) * scale * gain
    return jnp.minimum(jnp.maximum(result, -most), most).astype(held_as)


def setup_inputs(seed: int = 0) -> dict:
    keys = jax.random.split(jax.random.key(seed), 4)
    volume = normal_values(keys[0], (DEP, HT, WD, CH), 1.0, 6.0, ((0, 16), (3, 32)))
    cotangent = normal_values(keys[1], (DEP, HT, WD, CH), 1.0, 6.0, ((0, 16), (3, 32)))
    kernel = normal_values(keys[2], (CH, 27, CH), (27 * CH) ** -0.5, 0.0390625, ((0, 32),))
    return dict(volume=volume, cotangent=cotangent, kernel=kernel)


def tap_offsets():
    return [(a, b, c) for a in range(3) for b in range(3) for c in range(3)]


def reference(volume, cotangent, kernel):
    depth_all, height, width, chans = volume.shape
    padded = jnp.pad(volume, ((1, 1), (1, 1), (1, 1), (0, 0)))
    rows = depth_all * height * width
    pre = jnp.zeros((rows, chans), jnp.float32)
    for tap, (a, b, c) in enumerate(tap_offsets()):
        window = padded[a:a + depth_all, b:b + height, c:c + width, :].reshape(rows, chans)
        pre = pre + lax.dot_general(window, kernel[:, tap, :], (((1,), (1,)), ((), ())),
                                    preferred_element_type=jnp.float32)
    sig = jax.nn.sigmoid(pre)
    grad_out = cotangent.reshape(rows, chans).astype(jnp.float32)
    slope = (grad_out * sig * (1.0 + pre * (1.0 - sig))).astype(jnp.bfloat16)
    slope_vol = slope.reshape(depth_all, height, width, chans)

    def channel_block(total, index):
        block = lax.dynamic_slice_in_dim(slope_vol, index * CS, CS, 3)
        spread = jnp.pad(block, ((1, 1), (1, 1), (1, 1), (0, 0)))
        columns = jnp.concatenate(
            [spread[2 - a:2 - a + depth_all, 2 - b:2 - b + height, 2 - c:2 - c + width, :] for (a, b, c) in tap_offsets()],
            axis=3).reshape(rows, 27 * CS)
        taps_k = lax.dynamic_slice_in_dim(kernel, index * CS, CS, 0)
        taps_t = jnp.transpose(taps_k, (1, 0, 2)).reshape(27 * CS, chans)
        part = jnp.dot(columns, taps_t, preferred_element_type=jnp.float32).astype(jnp.bfloat16)
        part = lax.optimization_barrier(part)
        return total + part.astype(jnp.float32), None

    grad_total, _ = lax.scan(channel_block, jnp.zeros((rows, chans), jnp.float32),
                             jnp.arange(N_CHAN, dtype=jnp.int32))
    input_grad = grad_total.reshape(depth_all, height, width, chans).astype(jnp.bfloat16)

    def slab_block(total, index):
        framed = lax.dynamic_slice_in_dim(padded, index * DZ, DZ + 2, 0)
        local_slope = lax.dynamic_slice_in_dim(slope_vol, index * DZ, DZ, 0).reshape(DZ * height * width, chans)
        parts = []
        for (a, b, c) in tap_offsets():
            window = framed[a:a + DZ, b:b + height, c:c + width, :].reshape(DZ * height * width, chans)
            parts.append(lax.dot_general(local_slope, window, (((0,), (0,)), ((), ())),
                                         preferred_element_type=jnp.float32))
        part = jnp.stack(parts, 1).astype(jnp.bfloat16)
        part = lax.optimization_barrier(part)
        return total + part.astype(jnp.float32), None

    kernel_total, _ = lax.scan(slab_block, jnp.zeros((chans, 27, chans), jnp.float32),
                               jnp.arange(N_DEPTH, dtype=jnp.int32))
    kernel_grad = kernel_total.reshape(N_CHAN, CS, 27, chans)
    return input_grad, kernel_grad
```

```python
import functools

import jax
import jax.numpy as jnp
from jax import lax
from jax.experimental import pallas as pl
from jax.experimental.pallas import tpu as pltpu
from jax.sharding import PartitionSpec as P

MESH = pl.DeviceIdType.MESH
F32, BF16 = jnp.float32, jnp.bfloat16
ND, NX, NL, NZ, NK = 16, 4, 4, 8, 32
CS, SIDE, VOX, CH = 32, 16, 256, 1024
HALF, TAPS, O2 = 512, 27, 64
TROWS, TPAD = TAPS * O2, 28 * O2


def kernel_body(
    vol_hbm, cot_hbm, k_hbm, ig_ref, kg_ref,
    vin, cin, xt, xh, kx, ktmp, k2, kt, psend, prec, sl, ss, cm, og, rs, v2, xc, slb, acc,
    in_sem, k_send, k_recv, a_send, a_recv, p_send, p_recv, s_send, s_recv, n_send, n_recv,
    v_send, v_recv, f_send, r_send, r_recv,
):
    d, k = lax.axis_index("depth"), lax.axis_index("chan")
    x, zl = d // NL, d % NL
    y, zh, c, m = k // 4, (k // 2) % 2, k % 2, k // 2
    z, sib = zh * NL + zl, k + 1 - 2 * c
    khalf = k // 16
    self_a = khalf == c
    self_v = jnp.logical_and(zl % 2 == c, x // 2 == c)

    def remote(src, dst, ssem, rsem, dev):
        return pltpu.make_async_remote_copy(
            src_ref=src, dst_ref=dst, send_sem=ssem, recv_sem=rsem, device_id=dev,
            device_id_type=MESH,
        )

    def taken(ref, sem):
        pltpu.make_async_copy(ref, ref, sem).wait()

    vol_in = pltpu.make_async_copy(vol_hbm, vin, in_sem.at[0])
    cot_in = pltpu.make_async_copy(cot_hbm, cin, in_sem.at[1])
    k_in = pltpu.make_async_copy(
        k_hbm.at[:, :, pl.ds(pl.multiple_of(c * HALF, HALF), HALF)], kx.at[0], in_sem.at[2]
    )
    vol_in.start()
    cot_in.start()
    k_in.start()

    bar = pltpu.get_barrier_semaphore()

    def greet(dd, kk):
        pl.semaphore_signal(bar, inc=1, device_id=(dd, kk), device_id_type=MESH)

    @pl.loop(0, 16)
    def _(j):
        to, frm = 2 * j + khalf, 16 * c + j

        @pl.when(to != k)
        def _():
            greet(d, to)

        @pl.when(frm != k)
        def _():
            greet(d, frm)

    @pl.loop(1, ND)
    def _(j):
        greet((d + j) % ND, k)

    greet(d, sib)
    greet((d + 1) % ND, sib)
    greet((d + ND - 1) % ND, sib)
    odd = (z + c) % 2

    @pl.loop(0, 8)
    def _(j):
        xs, t = j // 2, j % 2
        step = jnp.where(odd == 1, 2 * t - 1, t * (2 - 4 * (xs % 2)))
        zs = (z - step + NZ) % NZ
        dd, kk = xs * NL + zs % NL, (y * 2 + zs // NL) * 2 + x // 2

        @pl.when(jnp.logical_or(dd != d, kk != k))
        def _():
            greet(dd, kk)

    vol_in.wait()
    xt[...] = vin[...].astype(F32).T.astype(BF16)

    zero = jnp.zeros((CS, VOX), BF16)
    slb[0] = jnp.zeros((3 * CS, VOX), BF16)
    slb[ND + 1] = jnp.zeros((3 * CS, VOX), BF16)
    sl[0] = zero
    sl[ND + 1] = zero
    cm[pl.ds(TROWS, O2), :] = jnp.zeros((O2, VOX), BF16)
    k2[pl.ds(TROWS, O2), :] = jnp.zeros((O2, HALF), BF16)

    @pl.when(d == 0)
    def _():
        prec[0] = jnp.zeros((2, CS, VOX), F32)
        ss[0] = zero

    @pl.when(d == ND - 1)
    def _():
        prec[2] = jnp.zeros((2, CS, VOX), F32)
        ss[2] = zero

    sa, sv = self_a.astype(jnp.int32), self_v.astype(jnp.int32)
    pl.semaphore_wait(bar, 2 * (16 - sa) + 15 + 3 + 8 - sv)

    a_slot = xh.at[pl.ds(pl.multiple_of((k % 16) * CS, CS), CS)]

    @pl.loop(0, 16)
    def _(j):
        to = 2 * ((m + j + 8) % 16) + khalf

        @pl.when(to != k)
        def _():
            remote(xt, a_slot, a_send, a_recv, (d, to)).start()

        @pl.when(to == k)
        def _():
            pltpu.make_async_copy(xt, a_slot, a_recv).start()

    k_out = remote(
        k_hbm.at[:, :, pl.ds(pl.multiple_of((1 - c) * HALF, HALF), HALF)], kx.at[1], k_send, k_recv,
        (d, sib),
    )
    k_out.start()

    def widen(r):
        @pl.loop(0, CS)
        def _(o):
            rows = kx[r, o].astype(F32)
            for g in range(4):
                ktmp[g, pl.ds(pl.multiple_of((r * CS + o) * 32, 32), TAPS), :] = rows[
                    :, g * 128 : g * 128 + 128
                ]

    k_in.wait()
    widen(0)
    k_out.wait_recv()
    widen(1)
    for t in range(TAPS):
        for g in range(4):
            k2[pl.ds(t * O2, O2), pl.ds(g * 128, 128)] = ktmp.at[g][
                pl.ds(t, O2, stride=32), :
            ].astype(BF16)
    for p in range(14):
        kt[:, pl.ds(p * 128, 128)] = k2[pl.ds(p * 128, 128), :].T

    lane = lax.broadcasted_iota(jnp.int32, (1, VOX), 1)
    hh, ww = lane // SIDE, lane % SIDE
    h_lo, h_hi = hh >= 1, hh <= SIDE - 2
    w_lo, w_hi = ww >= 1, ww <= SIDE - 2

    def moved(v, step, keep):
        return jnp.where(keep, pltpu.roll(v, step % VOX, 1), 0.0)

    def up(v):
        return moved(v, SIDE, h_lo)

    def down(v):
        return moved(v, -SIDE, h_hi)

    def right(v):
        return moved(v, 1, w_lo)

    def left(v):
        return moved(v, -1, w_hi)

    cin_t = None
    taken(xh, a_recv)
    xv = xh[...]

    for a in (0, 2, 1):
        yv = jnp.dot(k2[pl.ds(a * 9 * O2, 9 * O2), :], xv, preferred_element_type=F32)

        def tap(b, cc):
            at = (b * 3 + cc) * O2
            return yv[at : at + O2, :]

        cols = [tap(1, cc) + up(tap(0, cc)) + down(tap(2, cc)) for cc in range(3)]
        tot = cols[1] + right(cols[0]) + left(cols[2])
        psend[a, 0] = tot[:CS]
        psend[a, 1] = tot[CS:]
        if a == 1:
            remote(psend.at[1, 1], prec.at[1, c], p_send.at[2], p_recv.at[1, c], (d, sib)).start()
        else:
            i = 0 if a == 0 else 1
            there = d + 1 - a

            @pl.when(jnp.logical_and(there >= 0, there < ND))
            def _():
                for r, kk in ((0, k), (1, sib)):
                    remote(
                        psend.at[a, r], prec.at[a, c], p_send.at[3 + 2 * i + r], p_recv.at[a, c],
                        (there, kk),
                    ).start()

    @pl.loop(0, 8)
    def _(j):
        xd, t = 2 * c + j // 4, j % 4
        step = jnp.where(t == 3, 2 - 4 * (x % 2), t - 1)
        zd = (z + step + NZ) % NZ
        dd, kk = xd * NL + zd % NL, (y * 2 + zd // NL) * 2 + zl % 2
        src = xh.at[pl.ds(pl.multiple_of(((j // 4) * NL + zd % NL) * 64, 64), 64)]
        own = jnp.logical_and(dd == d, kk == k)

        @pl.when(jnp.logical_not(own))
        def _():
            remote(src, v2.at[d], v_send, v_recv.at[d], (dd, kk)).start()

        @pl.when(own)
        def _():
            pltpu.make_async_copy(src, v2.at[d], v_recv.at[d]).start()

    cot_in.wait()
    cot_t = cin[...].astype(F32).T
    not_first, not_last = d >= 1, d <= ND - 2
    taken(prec.at[1, 1 - c], p_recv.at[1, 1 - c])

    @pl.when(not_first)
    def _():
        taken(prec.at[0, 0], p_recv.at[0, 0])
        taken(prec.at[0, 1], p_recv.at[0, 1])

    @pl.when(not_last)
    def _():
        taken(prec.at[2, 0], p_recv.at[2, 0])
        taken(prec.at[2, 1], p_recv.at[2, 1])

    pre = psend[1, 0] + prec[1, 1 - c]
    pre = pre + (prec[0, 0] + prec[0, 1]) + (prec[2, 0] + prec[2, 1])
    sig = 1.0 / (1.0 + jnp.exp(-pre))
    sl[d + 1] = (cot_t * sig * (1.0 + pre * (1.0 - sig))).astype(BF16)

    mine = sl.at[d + 1]

    def slope_out(n):
        return remote(mine, mine, s_send.at[n], s_recv.at[d], ((d + n) % ND, k))

    slope_out(1).start()
    slope_out(ND - 1).start()
    remote(mine, ss.at[1], n_send.at[1], n_recv.at[1], (d, sib)).start()

    @pl.when(not_first)
    def _():
        remote(mine, ss.at[2], n_send.at[0], n_recv.at[2], (d - 1, sib)).start()

    @pl.when(not_last)
    def _():
        remote(mine, ss.at[0], n_send.at[2], n_recv.at[0], (d + 1, sib)).start()

    @pl.loop(2, ND - 1)
    def _(n):
        slope_out(n).start()

    taken(ss.at[1], n_recv.at[1])

    @pl.when(not_first)
    def _():
        taken(sl.at[d], s_recv.at[d - 1])
        taken(ss.at[0], n_recv.at[0])

    @pl.when(not_last)
    def _():
        taken(sl.at[d + 2], s_recv.at[d + 1])
        taken(ss.at[2], n_recv.at[2])

    for a in (1, 0, 2):
        s = jnp.concatenate([sl[d + 2 - a], ss[2 - a]], axis=0).astype(F32)
        for cc, sc in ((1, s), (0, left(s)), (2, right(s))):
            for b, sb in ((1, sc), (0, down(sc)), (2, up(sc))):
                cm[pl.ds((a * 9 + b * 3 + cc) * O2, O2), :] = sb.astype(BF16)

    r_slot = rs.at[m]

    @pl.loop(0, 4)
    def _(q):
        rows = pl.ds(pl.multiple_of(q * 128, 128), 128)
        og[rows, :] = jnp.dot(kt[rows, :], cm[...], preferred_element_type=F32).astype(BF16)

        @pl.loop(0, 4)
        def _(i):
            j = q * 4 + i
            to = 16 * c + j
            src = og.at[pl.ds(pl.multiple_of(j * CS, CS), CS)]

            @pl.when(to != k)
            def _():
                remote(src, r_slot, r_send, r_recv, (d, to)).start()

            @pl.when(to == k)
            def _():
                pltpu.make_async_copy(src, r_slot, r_recv).start()

    @pl.loop(0, 8)
    def _(j):
        p = (j // 2) * NL + 2 * (j % 2) + c
        taken(v2.at[p], v_recv.at[p])
        remote(v2.at[p], v2.at[p], f_send, v_recv.at[p], (d, sib)).start()

    @pl.loop(0, 8)
    def _(j):
        p = (j // 2) * NL + 2 * (j % 2) + 1 - c
        taken(v2.at[p], v_recv.at[p])

    @pl.loop(0, ND)
    def _(p):
        v = v2[p].astype(F32)
        xc[p, pl.ds(0, 64), :] = right(v).astype(BF16)
        xc[p, pl.ds(64, 64), :] = v2[p]
        xc[p, pl.ds(128, 64), :] = left(v).astype(BF16)

    @pl.loop(0, ND)
    def _(p):
        @pl.when(jnp.logical_or(p < d - 1, p > d + 1))
        def _():
            taken(sl.at[p + 1], s_recv.at[p])

    @pl.loop(0, ND)
    def _(p):
        v = sl[p + 1].astype(F32)
        slb[p + 1, pl.ds(0, CS), :] = down(v).astype(BF16)
        slb[p + 1, pl.ds(CS, CS), :] = sl[p + 1]
        slb[p + 1, pl.ds(2 * CS, CS), :] = up(v).astype(BF16)

    acc[...] = jnp.zeros((9 * CS, 192), F32)

    @pl.loop(0, ND)
    def _(p):
        lhs = slb[pl.ds(p, 3)].reshape(9 * CS, VOX)
        acc[...] += lax.dot_general(
            lhs, xc[p], (((1,), (1,)), ((), ())), preferred_element_type=F32
        )

    for a in range(3):
        for b in range(3):
            rows = acc[pl.ds(((2 - a) * 3 + b) * CS, CS), :]
            for cc in range(3):
                part = rows[:, cc * 64 : cc * 64 + 64]
                kg_ref[pl.ds(a * 9 + b * 3 + cc, CS, stride=32), :] = jnp.concatenate(
                    [part, part], axis=1
                )

    taken(rs, r_recv)
    total = rs[0].astype(F32)
    for j in range(1, 16):
        total = total + rs[j].astype(F32)
    ig_ref[...] = total.T.astype(BF16)

    k_out.wait_send()
    for own, sem in ((self_a, a_send), (self_a, r_send)):
        @pl.when(own)
        def _():
            taken(xh.at[pl.ds(0, 15 * CS)], sem)

        @pl.when(jnp.logical_not(own))
        def _():
            taken(xh, sem)

    @pl.when(self_v)
    def _():
        taken(v2.at[pl.ds(0, 7)], v_send)

    @pl.when(jnp.logical_not(self_v))
    def _():
        taken(v2.at[pl.ds(0, 8)], v_send)

    taken(v2.at[pl.ds(0, 8)], f_send)
    taken(psend.at[1, 1], p_send.at[2])

    @pl.when(not_last)
    def _():
        for r in range(2):
            taken(psend.at[0, r], p_send.at[3 + r])
        taken(mine, n_send.at[2])

    @pl.when(not_first)
    def _():
        for r in range(2):
            taken(psend.at[2, r], p_send.at[5 + r])
        taken(mine, n_send.at[0])

    taken(mine, n_send.at[1])

    @pl.loop(1, ND)
    def _(n):
        taken(mine, s_send.at[n])


def local(volume, cotangent, kernel):
    any_space = pl.BlockSpec(memory_space=pl.ANY)
    in_vmem = pl.BlockSpec(memory_space=pltpu.VMEM)
    dma = pltpu.SemaphoreType.DMA
    ig, kg = pl.pallas_call(
        kernel_body,
        out_shape=(
            jax.ShapeDtypeStruct((VOX, CS), BF16),
            jax.ShapeDtypeStruct((CS * 32, 128), F32),
        ),
        in_specs=[any_space] * 3,
        out_specs=(in_vmem, in_vmem),
        scratch_shapes=[
            pltpu.VMEM((VOX, CS), BF16),
            pltpu.VMEM((VOX, CS), BF16),
            pltpu.VMEM((CS, VOX), BF16),
            pltpu.VMEM((HALF, VOX), BF16),
            pltpu.VMEM((2, CS, TAPS, HALF), BF16),
            pltpu.VMEM((4, O2 * 32, 128), F32),
            pltpu.VMEM((TPAD, HALF), BF16),
            pltpu.VMEM((HALF, TPAD), BF16),
            pltpu.VMEM((3, 2, CS, VOX), F32),
            pltpu.VMEM((3, 2, CS, VOX), F32),
            pltpu.VMEM((ND + 2, CS, VOX), BF16),
            pltpu.VMEM((3, CS, VOX), BF16),
            pltpu.VMEM((TPAD, VOX), BF16),
            pltpu.VMEM((HALF, VOX), BF16),
            pltpu.VMEM((16, CS, VOX), BF16),
            pltpu.VMEM((ND, 64, VOX), BF16),
            pltpu.VMEM((ND, 192, VOX), BF16),
            pltpu.VMEM((ND + 2, 3 * CS, VOX), BF16),
            pltpu.VMEM((9 * CS, 192), F32),
            dma((3,)), dma, dma, dma, dma, dma((7,)), dma((3, 2)), dma((ND,)), dma((ND,)),
            dma((3,)), dma((3,)), dma, dma((ND,)), dma, dma, dma,
        ],
        compiler_params=pltpu.CompilerParams(
            collective_id=0, has_side_effects=True, vmem_limit_bytes=40 * 2**20
        ),
        cost_estimate=pl.CostEstimate(
            flops=3 * 453_000_000, bytes_accessed=6_000_000, transcendentals=8192
        ),
    )(volume.reshape(VOX, CS), cotangent.reshape(VOX, CS), kernel)
    input_grad = ig.reshape(1, SIDE, SIDE, CS)
    kernel_grad = kg.reshape(1, CS, 32, 128)[:, :, :TAPS, :64]
    return (input_grad, kernel_grad)


def solution(mesh):
    return jax.shard_map(
        local,
        mesh=mesh,
        in_specs=(
            P("depth", None, None, "chan"),
            P("depth", None, None, "chan"),
            P("chan", None, None),
        ),
        out_specs=(P("depth", None, None, "chan"), P("chan", None, None, "depth")),
        check_vma=False,
    )
```

```python
import functools

import jax
import jax.numpy as jnp
from jax import lax
from jax.experimental import pallas as pl
from jax.experimental.pallas import tpu as pltpu
from jax.sharding import PartitionSpec as P

MESH = pl.DeviceIdType.MESH
F32, BF16 = jnp.float32, jnp.bfloat16
ND, NX, NL, NZ, NK = 16, 4, 4, 8, 32
CS, SIDE, VOX, CH = 32, 16, 256, 1024
HALF, TAPS, O2 = 512, 27, 64
TROWS, TPAD = TAPS * O2, 28 * O2


def finish(ig_ref, kg_ref, ig_out, kg_out, sem):
    a = pltpu.make_async_copy(ig_ref, ig_out, sem.at[0])
    b = pltpu.make_async_copy(kg_ref, kg_out, sem.at[1])
    b.start()
    a.start()
    a.wait()
    b.wait()


def kernel_body(
    vol_hbm, cot_hbm, k_hbm, ig_ref, kg_ref,
    vin, cin, xt, xh, k2, kt, psend, prec, held, sl, ss, cm, og, rs, v2, xc, slb, acc,
    in_sem, k_send, k_recv, a_send, a_recv, p_send, p_recv, s_send, s_recv, n_send, n_recv,
    v_send, v_recv, f_send, r_send, r_recv,
):
    d, k = lax.axis_index("depth"), lax.axis_index("chan")
    x, zl = d // NL, d % NL
    y, zh, c, m = k // 4, (k // 2) % 2, k % 2, k // 2
    z, sib = zh * NL + zl, k + 1 - 2 * c
    khalf = k // 16
    self_a = khalf == c
    self_v = jnp.logical_and(zl % 2 == c, x // 2 == c)

    def remote(src, dst, ssem, rsem, dev):
        return pltpu.make_async_remote_copy(
            src_ref=src, dst_ref=dst, send_sem=ssem, recv_sem=rsem, device_id=dev,
            device_id_type=MESH,
        )

    def taken(ref, sem):
        pltpu.make_async_copy(ref, ref, sem).wait()

    vol_in = pltpu.make_async_copy(vol_hbm, vin, in_sem.at[0])
    cot_in = pltpu.make_async_copy(cot_hbm, cin, in_sem.at[1])
    k_in = pltpu.make_async_copy(
        k_hbm.at[:, :, pl.ds(pl.multiple_of(c * HALF, HALF), HALF)],
        k2.at[pl.ds(0, TAPS), pl.ds(0, CS)], in_sem.at[2],
    )
    vol_in.start()
    cot_in.start()
    k_in.start()

    bar = pltpu.get_barrier_semaphore()

    def greet(dd, kk):
        pl.semaphore_signal(bar, inc=1, device_id=(dd, kk), device_id_type=MESH)

    def far_first(j):
        i = j // 2
        dy = 4 + jnp.where(i % 2 == 1, -((i + 1) // 2), i // 2)
        yy = (y + dy) % 8
        return yy, yy * 2 + jnp.where(j % 2 == 0, 1 - zh, zh)

    @pl.loop(0, 16)
    def _(j):
        yy, mm = far_first(j)
        mine = 2 * mm + khalf

        @pl.when(mine != k)
        def _():
            greet(d, mine)

        @pl.when(jnp.logical_and(yy // 4 == c, mine + 1 - 2 * khalf != k))
        def _():
            greet(d, mine + 1 - 2 * khalf)

    @pl.loop(1, ND)
    def _(j):
        greet((d + j) % ND, k)

    greet((d + 1) % ND, sib)
    greet((d + ND - 1) % ND, sib)
    odd = (z + c) % 2

    @pl.loop(0, 8)
    def _(j):
        xs, t = j // 2, j % 2
        step = jnp.where(odd == 1, 2 * t - 1, t * (2 - 4 * (xs % 2)))
        zs = (z - step + NZ) % NZ
        dd, kk = xs * NL + zs % NL, (y * 2 + zs // NL) * 2 + x // 2

        @pl.when(jnp.logical_or(dd != d, kk != k))
        def _():
            greet(dd, kk)

    vol_in.wait()
    xt[...] = vin[...].astype(F32).T.astype(BF16)

    zero = jnp.zeros((CS, VOX), BF16)
    slb[0] = jnp.zeros((3 * CS, VOX), BF16)
    slb[ND + 1] = jnp.zeros((3 * CS, VOX), BF16)
    sl[0] = zero
    sl[ND + 1] = zero
    cm[pl.ds(TROWS, O2), :] = jnp.zeros((O2, VOX), BF16)
    k2[TAPS] = jnp.zeros((O2, HALF), BF16)

    @pl.when(d == 0)
    def _():
        prec[0] = jnp.zeros((2, CS, VOX), BF16)
        ss[0] = zero

    @pl.when(d == ND - 1)
    def _():
        prec[2] = jnp.zeros((2, CS, VOX), BF16)
        ss[2] = zero

    sa, sv = self_a.astype(jnp.int32), self_v.astype(jnp.int32)
    pl.semaphore_wait(bar, 24 - sa + 15 + 2 + 8 - sv)

    a_slot = xh.at[pl.ds(pl.multiple_of((k % 16) * CS, CS), CS)]

    @pl.loop(0, 16)
    def _(j):
        to = 2 * far_first(j)[1] + khalf

        @pl.when(to != k)
        def _():
            remote(xt, a_slot, a_send, a_recv, (d, to)).start()

        @pl.when(to == k)
        def _():
            pltpu.make_async_copy(xt, a_slot, a_recv).start()

    k_out = remote(
        k_hbm.at[:, :, pl.ds(pl.multiple_of((1 - c) * HALF, HALF), HALF)],
        k2.at[pl.ds(0, TAPS), pl.ds(CS, CS)], k_send, k_recv, (d, sib),
    )
    k_out.start()

    k_in.wait()
    k_out.wait_recv()
    for p in range(14):
        kt[:, pl.ds(p * 128, 128)] = k2[pl.ds(2 * p, 2)].reshape(128, HALF).T

    lane = lax.broadcasted_iota(jnp.int32, (1, VOX), 1)
    hh, ww = lane // SIDE, lane % SIDE
    h_lo, h_hi = hh >= 1, hh <= SIDE - 2
    w_lo, w_hi = ww >= 1, ww <= SIDE - 2

    def moved(v, step, keep):
        return jnp.where(keep, pltpu.roll(v, step % VOX, 1), 0.0)

    def up(v):
        return moved(v, SIDE, h_lo)

    def down(v):
        return moved(v, -SIDE, h_hi)

    def right(v):
        return moved(v, 1, w_lo)

    def left(v):
        return moved(v, -1, w_hi)

    taken(xh, a_recv)
    xv = xh[...]

    for a in (0, 2, 1):
        yv = jnp.dot(k2[pl.ds(a * 9, 9)].reshape(9 * O2, HALF), xv, preferred_element_type=F32)

        def tap(b, cc):
            at = (b * 3 + cc) * O2
            return yv[at : at + O2, :]

        cols = [tap(1, cc) + up(tap(0, cc)) + down(tap(2, cc)) for cc in range(3)]
        tot = cols[1] + right(cols[0]) + left(cols[2])
        if a == 1:
            held[...] = tot[:CS]
            psend[a, 1] = tot[CS:].astype(BF16)
            remote(psend.at[1, 1], prec.at[1, c], p_send.at[2], p_recv.at[1, c], (d, sib)).start()
        else:
            psend[a, 0] = tot[:CS].astype(BF16)
            psend[a, 1] = tot[CS:].astype(BF16)
            i = 0 if a == 0 else 1
            there = d + 1 - a

            @pl.when(jnp.logical_and(there >= 0, there < ND))
            def _():
                for r, kk in ((0, k), (1, sib)):
                    remote(
                        psend.at[a, r], prec.at[a, c], p_send.at[3 + 2 * i + r], p_recv.at[a, c],
                        (there, kk),
                    ).start()

    @pl.loop(0, 8)
    def _(j):
        xd, t = 2 * c + j // 4, j % 4
        step = jnp.where(t == 3, 2 - 4 * (x % 2), t - 1)
        zd = (z + step + NZ) % NZ
        dd, kk = xd * NL + zd % NL, (y * 2 + zd // NL) * 2 + zl % 2
        src = xh.at[pl.ds(pl.multiple_of(((j // 4) * NL + zd % NL) * 64, 64), 64)]
        own = jnp.logical_and(dd == d, kk == k)

        @pl.when(jnp.logical_not(own))
        def _():
            remote(src, v2.at[d], v_send, v_recv.at[d], (dd, kk)).start()

        @pl.when(own)
        def _():
            pltpu.make_async_copy(src, v2.at[d], v_recv.at[d]).start()

    cot_in.wait()
    cot_t = cin[...].astype(F32).T
    not_first, not_last = d >= 1, d <= ND - 2
    taken(prec.at[1, 1 - c], p_recv.at[1, 1 - c])

    @pl.when(not_first)
    def _():
        taken(prec.at[0, 0], p_recv.at[0, 0])
        taken(prec.at[0, 1], p_recv.at[0, 1])

    @pl.when(not_last)
    def _():
        taken(prec.at[2, 0], p_recv.at[2, 0])
        taken(prec.at[2, 1], p_recv.at[2, 1])

    got = [prec[1, 1 - c], prec[0, 0], prec[0, 1], prec[2, 0], prec[2, 1]]
    pre = held[...] + sum(v.astype(F32) for v in got)
    sig = 1.0 / (1.0 + jnp.exp(-pre))
    sl[d + 1] = (cot_t * sig * (1.0 + pre * (1.0 - sig))).astype(BF16)

    mine = sl.at[d + 1]

    def slope_out(n):
        return remote(mine, mine, s_send.at[n], s_recv.at[d], ((d + n) % ND, k))

    slope_out(1).start()
    slope_out(ND - 1).start()
    remote(mine, ss.at[1], n_send.at[1], n_recv.at[1], (d, sib)).start()

    @pl.when(not_first)
    def _():
        remote(mine, ss.at[2], n_send.at[0], n_recv.at[2], (d - 1, sib)).start()

    @pl.when(not_last)
    def _():
        remote(mine, ss.at[0], n_send.at[2], n_recv.at[0], (d + 1, sib)).start()

    @pl.loop(2, ND - 1)
    def _(n):
        slope_out(n).start()

    taken(ss.at[1], n_recv.at[1])

    @pl.when(not_first)
    def _():
        taken(sl.at[d], s_recv.at[d - 1])
        taken(ss.at[0], n_recv.at[0])

    @pl.when(not_last)
    def _():
        taken(sl.at[d + 2], s_recv.at[d + 1])
        taken(ss.at[2], n_recv.at[2])

    for a in (1, 0, 2):
        s = jnp.concatenate([sl[d + 2 - a], ss[2 - a]], axis=0).astype(F32)
        for cc, sc in ((1, s), (0, left(s)), (2, right(s))):
            for b, sb in ((1, sc), (0, down(sc)), (2, up(sc))):
                cm[pl.ds((a * 9 + b * 3 + cc) * O2, O2), :] = sb.astype(BF16)

    r_slot = rs.at[m]

    near = jnp.where(khalf == c, 2, 0)

    @pl.loop(0, 4)
    def _(n):
        q = (y + n + near) % 4
        rows = pl.ds(pl.multiple_of(q * 128, 128), 128)
        og[rows, :] = jnp.dot(kt[rows, :], cm[...], preferred_element_type=F32).astype(BF16)

        @pl.loop(0, 4)
        def _(i):
            j = q * 4 + i
            to = 16 * c + j
            src = og.at[pl.ds(pl.multiple_of(j * CS, CS), CS)]

            @pl.when(to != k)
            def _():
                remote(src, r_slot, r_send, r_recv, (d, to)).start()

            @pl.when(to == k)
            def _():
                pltpu.make_async_copy(src, r_slot, r_recv).start()

    def spread_chans(odd_plane, forward):
        @pl.loop(0, 8)
        def _(j):
            p = (j // 2) * NL + 2 * (j % 2) + odd_plane
            taken(v2.at[p], v_recv.at[p])
            if forward:
                remote(v2.at[p], v2.at[p], f_send, v_recv.at[p], (d, sib)).start()
            v = v2[p].astype(F32)
            xc[p, pl.ds(0, 64), :] = right(v).astype(BF16)
            xc[p, pl.ds(64, 64), :] = v2[p]
            xc[p, pl.ds(128, 64), :] = left(v).astype(BF16)

    spread_chans(c, True)

    spread_chans(1 - c, False)

    @pl.loop(0, ND)
    def _(p):
        @pl.when(jnp.logical_or(p < d - 1, p > d + 1))
        def _():
            taken(sl.at[p + 1], s_recv.at[p])

    @pl.loop(0, ND)
    def _(p):
        v = sl[p + 1].astype(F32)
        slb[p + 1, pl.ds(0, CS), :] = down(v).astype(BF16)
        slb[p + 1, pl.ds(CS, CS), :] = sl[p + 1]
        slb[p + 1, pl.ds(2 * CS, CS), :] = up(v).astype(BF16)

    acc[...] = jnp.zeros((9 * CS, 192), F32)

    @pl.loop(0, ND)
    def _(p):
        lhs = slb[pl.ds(p, 3)].reshape(9 * CS, VOX)
        acc[...] += lax.dot_general(
            lhs, xc[p], (((1,), (1,)), ((), ())), preferred_element_type=F32
        )

    for a in range(3):
        for b in range(3):
            rows = acc[pl.ds(((2 - a) * 3 + b) * CS, CS), :]
            for cc in range(3):
                part = rows[:, cc * 64 : cc * 64 + 64]
                kg_ref[a * 9 + b * 3 + cc] = part

    taken(rs, r_recv)
    total = rs[0].astype(F32)
    for j in range(1, 16):
        total = total + rs[j].astype(F32)
    ig_ref[...] = total.T.astype(BF16)

    k_out.wait_send()
    for own, sem in ((self_a, a_send), (self_a, r_send)):
        @pl.when(own)
        def _():
            taken(xh.at[pl.ds(0, 15 * CS)], sem)

        @pl.when(jnp.logical_not(own))
        def _():
            taken(xh, sem)

    @pl.when(self_v)
    def _():
        taken(v2.at[pl.ds(0, 7)], v_send)

    @pl.when(jnp.logical_not(self_v))
    def _():
        taken(v2.at[pl.ds(0, 8)], v_send)

    taken(v2.at[pl.ds(0, 8)], f_send)
    taken(psend.at[1, 1], p_send.at[2])

    @pl.when(not_last)
    def _():
        for r in range(2):
            taken(psend.at[0, r], p_send.at[3 + r])
        taken(mine, n_send.at[2])

    @pl.when(not_first)
    def _():
        for r in range(2):
            taken(psend.at[2, r], p_send.at[5 + r])
        taken(mine, n_send.at[0])

    taken(mine, n_send.at[1])

    @pl.loop(1, ND)
    def _(n):
        taken(mine, s_send.at[n])


def local(volume, cotangent, kernel):
    in_hbm = pl.BlockSpec(memory_space=pltpu.HBM)
    in_vmem = pl.BlockSpec(memory_space=pltpu.VMEM)
    dma = pltpu.SemaphoreType.DMA
    ig, kg = pl.pallas_call(
        kernel_body,
        out_shape=(
            jax.ShapeDtypeStruct((VOX, CS), BF16),
            jax.ShapeDtypeStruct((TAPS, CS, 64), F32),
        ),
        in_specs=[in_hbm] * 3,
        out_specs=(in_vmem, in_vmem),
        scratch_shapes=[
            pltpu.VMEM((VOX, CS), BF16),
            pltpu.VMEM((VOX, CS), BF16),
            pltpu.VMEM((CS, VOX), BF16),
            pltpu.VMEM((HALF, VOX), BF16),
                    pltpu.VMEM((28, O2, HALF), BF16),
            pltpu.VMEM((HALF, TPAD), BF16),
            pltpu.VMEM((3, 2, CS, VOX), BF16),
            pltpu.VMEM((3, 2, CS, VOX), BF16),
            pltpu.VMEM((CS, VOX), F32),
            pltpu.VMEM((ND + 2, CS, VOX), BF16),
            pltpu.VMEM((3, CS, VOX), BF16),
            pltpu.VMEM((TPAD, VOX), BF16),
            pltpu.VMEM((HALF, VOX), BF16),
            pltpu.VMEM((16, CS, VOX), BF16),
            pltpu.VMEM((ND, 64, VOX), BF16),
            pltpu.VMEM((ND, 192, VOX), BF16),
            pltpu.VMEM((ND + 2, 3 * CS, VOX), BF16),
            pltpu.VMEM((9 * CS, 192), F32),
            dma((3,)), dma, dma, dma, dma, dma((7,)), dma((3, 2)), dma((ND,)), dma((ND,)),
            dma((3,)), dma((3,)), dma, dma((ND,)), dma, dma, dma,
        ],
        compiler_params=pltpu.CompilerParams(
            collective_id=0, has_side_effects=True, vmem_limit_bytes=48 * 2**20
        ),
        cost_estimate=pl.CostEstimate(
            flops=3 * 453_000_000, bytes_accessed=6_000_000, transcendentals=8192
        ),
    )(
        pltpu.with_memory_space_constraint(volume.reshape(VOX, CS), pltpu.HBM),
        pltpu.with_memory_space_constraint(cotangent.reshape(VOX, CS), pltpu.HBM),
        pltpu.with_memory_space_constraint(jnp.transpose(kernel, (1, 0, 2)), pltpu.HBM),
    )
    ig, kg = pl.pallas_call(
        finish,
        out_shape=(
            jax.ShapeDtypeStruct((VOX, CS), BF16),
            jax.ShapeDtypeStruct((TAPS, CS, 64), F32),
        ),
        in_specs=[pl.BlockSpec(memory_space=pl.ANY)] * 2,
        out_specs=(pl.BlockSpec(memory_space=pl.ANY),) * 2,
        scratch_shapes=[dma((2,))],
    )(*(pltpu.with_memory_space_constraint(v, pltpu.VMEM) for v in (ig, kg)))
    input_grad = ig.reshape(1, SIDE, SIDE, CS)
    kernel_grad = jnp.transpose(kg, (1, 0, 2))[None]
    return (input_grad, kernel_grad)


def solution(mesh):
    return jax.shard_map(
        local,
        mesh=mesh,
        in_specs=(
            P("depth", None, None, "chan"),
            P("depth", None, None, "chan"),
            P("chan", None, None),
        ),
        out_specs=(P("depth", None, None, "chan"), P("chan", None, None, "depth")),
        check_vma=False,
    )
```

```python
import functools

import jax
import jax.numpy as jnp
from jax import lax
from jax.experimental import pallas as pl
from jax.experimental.pallas import tpu as pltpu
from jax.sharding import PartitionSpec as P

MESH = pl.DeviceIdType.MESH
F32, BF16 = jnp.float32, jnp.bfloat16
ND, NX, NL, NZ, NK = 16, 4, 4, 8, 32
CS, SIDE, VOX, CH = 32, 16, 256, 1024
HALF, TAPS, O2 = 512, 27, 64
TROWS, TPAD = TAPS * O2, 28 * O2


def finish(ig_ref, kg_ref, ig_out, kg_out, sem):
    a = pltpu.make_async_copy(ig_ref, ig_out, sem.at[0])
    b = pltpu.make_async_copy(kg_ref, kg_out, sem.at[1])
    b.start()
    a.start()
    a.wait()
    b.wait()


def kernel_body(
    vol_hbm, cot_hbm, k_hbm, ig_ref, kg_ref,
    vin, cin, xt, xh, k2, kt, psend, prec, held, sl, ss, cm, og, rs, v2, xc, slb, acc,
    in_sem, k_send, k_recv, a_send, a_recv, p_send, p_recv, s_send, s_recv, n_send, n_recv,
    v_send, v_recv, f_send, r_send, r_recv,
):
    d, k = lax.axis_index("depth"), lax.axis_index("chan")
    x, zl = d // NL, d % NL
    y, zh, c, m = k // 4, (k // 2) % 2, k % 2, k // 2
    z, sib = zh * NL + zl, k + 1 - 2 * c
    khalf = k // 16
    self_a = khalf == c
    self_v = jnp.logical_and(zl % 2 == c, x // 2 == c)

    def remote(src, dst, ssem, rsem, dev):
        return pltpu.make_async_remote_copy(
            src_ref=src, dst_ref=dst, send_sem=ssem, recv_sem=rsem, device_id=dev,
            device_id_type=MESH,
        )

    def taken(ref, sem):
        pltpu.make_async_copy(ref, ref, sem).wait()

    vol_in = pltpu.make_async_copy(vol_hbm, vin, in_sem.at[0])
    cot_in = pltpu.make_async_copy(cot_hbm, cin, in_sem.at[1])
    k_in = pltpu.make_async_copy(
        k_hbm.at[:, :, pl.ds(pl.multiple_of(c * HALF, HALF), HALF)],
        k2.at[pl.ds(0, TAPS), pl.ds(0, CS)], in_sem.at[2],
    )
    vol_in.start()
    cot_in.start()
    k_in.start()

    bar = pltpu.get_barrier_semaphore()

    def greet(dd, kk):
        pl.semaphore_signal(bar, inc=1, device_id=(dd, kk), device_id_type=MESH)

    def far_first(j):
        i = j % 8
        dy = 4 + jnp.where(i % 2 == 1, -((i + 1) // 2), i // 2)
        yy = (y + dy) % 8
        return yy, yy * 2 + jnp.where(j < 8, 1 - zh, zh)

    @pl.loop(0, 16)
    def _(j):
        yy, mm = far_first(j)
        mine = 2 * mm + khalf

        @pl.when(mine != k)
        def _():
            greet(d, mine)

        @pl.when(jnp.logical_and(yy // 4 == c, mine + 1 - 2 * khalf != k))
        def _():
            greet(d, mine + 1 - 2 * khalf)

    @pl.loop(1, ND)
    def _(j):
        greet((d + j) % ND, k)

    greet((d + 1) % ND, sib)
    greet((d + ND - 1) % ND, sib)
    odd = (z + c) % 2

    @pl.loop(0, 8)
    def _(j):
        xs, t = j // 2, j % 2
        step = jnp.where(odd == 1, 2 * t - 1, t * (2 - 4 * (xs % 2)))
        zs = (z - step + NZ) % NZ
        dd, kk = xs * NL + zs % NL, (y * 2 + zs // NL) * 2 + x // 2

        @pl.when(jnp.logical_or(dd != d, kk != k))
        def _():
            greet(dd, kk)

    vol_in.wait()
    xt[...] = vin[...].astype(F32).T.astype(BF16)

    zero = jnp.zeros((CS, VOX), BF16)
    slb[0] = jnp.zeros((3 * CS, VOX), BF16)
    slb[ND + 1] = jnp.zeros((3 * CS, VOX), BF16)
    sl[0] = zero
    sl[ND + 1] = zero
    cm[pl.ds(TROWS, O2), :] = jnp.zeros((O2, VOX), BF16)
    k2[TAPS] = jnp.zeros((O2, HALF), BF16)

    @pl.when(d == 0)
    def _():
        prec[0] = jnp.zeros((2, CS, VOX), BF16)
        ss[0] = zero

    @pl.when(d == ND - 1)
    def _():
        prec[2] = jnp.zeros((2, CS, VOX), BF16)
        ss[2] = zero

    sa, sv = self_a.astype(jnp.int32), self_v.astype(jnp.int32)
    pl.semaphore_wait(bar, 24 - sa + 15 + 2 + 8 - sv)

    a_slot = xh.at[pl.ds(pl.multiple_of((k % 16) * CS, CS), CS)]

    @pl.loop(0, 16)
    def _(j):
        to = 2 * far_first(j)[1] + khalf

        @pl.when(to != k)
        def _():
            remote(xt, a_slot, a_send, a_recv, (d, to)).start()

        @pl.when(to == k)
        def _():
            pltpu.make_async_copy(xt, a_slot, a_recv).start()

    k_out = remote(
        k_hbm.at[:, :, pl.ds(pl.multiple_of((1 - c) * HALF, HALF), HALF)],
        k2.at[pl.ds(0, TAPS), pl.ds(CS, CS)], k_send, k_recv, (d, sib),
    )
    k_out.start()

    k_in.wait()
    k_out.wait_recv()
    for p in range(14):
        kt[:, pl.ds(p * 128, 128)] = k2[pl.ds(2 * p, 2)].reshape(128, HALF).T

    lane = lax.broadcasted_iota(jnp.int32, (1, VOX), 1)
    hh, ww = lane // SIDE, lane % SIDE
    h_lo, h_hi = hh >= 1, hh <= SIDE - 2
    w_lo, w_hi = ww >= 1, ww <= SIDE - 2

    def moved(v, step, keep):
        return jnp.where(keep, pltpu.roll(v, step % VOX, 1), 0.0)

    def up(v):
        return moved(v, SIDE, h_lo)

    def down(v):
        return moved(v, -SIDE, h_hi)

    def right(v):
        return moved(v, 1, w_lo)

    def left(v):
        return moved(v, -1, w_hi)

    taken(xh, a_recv)
    xv = xh[...]

    for a in (0, 2, 1):
        yv = jnp.dot(k2[pl.ds(a * 9, 9)].reshape(9 * O2, HALF), xv, preferred_element_type=F32)

        def tap(b, cc):
            at = (b * 3 + cc) * O2
            return yv[at : at + O2, :]

        cols = [tap(1, cc) + up(tap(0, cc)) + down(tap(2, cc)) for cc in range(3)]
        tot = cols[1] + right(cols[0]) + left(cols[2])
        if a == 1:
            held[...] = tot[:CS]
            psend[a, 1] = tot[CS:].astype(BF16)
            remote(psend.at[1, 1], prec.at[1, c], p_send.at[2], p_recv.at[1, c], (d, sib)).start()
        else:
            psend[a, 0] = tot[:CS].astype(BF16)
            psend[a, 1] = tot[CS:].astype(BF16)
            i = 0 if a == 0 else 1
            there = d + 1 - a

            @pl.when(jnp.logical_and(there >= 0, there < ND))
            def _():
                for r, kk in ((0, k), (1, sib)):
                    remote(
                        psend.at[a, r], prec.at[a, c], p_send.at[3 + 2 * i + r], p_recv.at[a, c],
                        (there, kk),
                    ).start()

    @pl.loop(0, 8)
    def _(j):
        xd, t = 2 * c + j % 2, j // 2
        step = jnp.where(t == 0, 2 - 4 * (x % 2), jnp.where(t == 3, 0, 2 * t - 3))
        zd = (z + step + NZ) % NZ
        dd, kk = xd * NL + zd % NL, (y * 2 + zd // NL) * 2 + zl % 2
        src = xh.at[pl.ds(pl.multiple_of(((j % 2) * NL + zd % NL) * 64, 64), 64)]
        own = jnp.logical_and(dd == d, kk == k)

        @pl.when(jnp.logical_not(own))
        def _():
            remote(src, v2.at[d], v_send, v_recv.at[d], (dd, kk)).start()

        @pl.when(own)
        def _():
            pltpu.make_async_copy(src, v2.at[d], v_recv.at[d]).start()

    cot_in.wait()
    cot_t = cin[...].astype(F32).T
    not_first, not_last = d >= 1, d <= ND - 2
    taken(prec.at[1, 1 - c], p_recv.at[1, 1 - c])

    @pl.when(not_first)
    def _():
        taken(prec.at[0, 0], p_recv.at[0, 0])
        taken(prec.at[0, 1], p_recv.at[0, 1])

    @pl.when(not_last)
    def _():
        taken(prec.at[2, 0], p_recv.at[2, 0])
        taken(prec.at[2, 1], p_recv.at[2, 1])

    got = [prec[1, 1 - c], prec[0, 0], prec[0, 1], prec[2, 0], prec[2, 1]]
    pre = held[...] + sum(v.astype(F32) for v in got)
    sig = 1.0 / (1.0 + jnp.exp(-pre))
    sl[d + 1] = (cot_t * sig * (1.0 + pre * (1.0 - sig))).astype(BF16)

    mine = sl.at[d + 1]

    def slope_out(n):
        return remote(mine, mine, s_send.at[n], s_recv.at[d], ((d + n) % ND, k))

    slope_out(1).start()
    slope_out(ND - 1).start()
    remote(mine, ss.at[1], n_send.at[1], n_recv.at[1], (d, sib)).start()

    @pl.when(not_first)
    def _():
        remote(mine, ss.at[2], n_send.at[0], n_recv.at[2], (d - 1, sib)).start()

    @pl.when(not_last)
    def _():
        remote(mine, ss.at[0], n_send.at[2], n_recv.at[0], (d + 1, sib)).start()

    @pl.loop(2, ND - 1)
    def _(n):
        slope_out(n).start()

    taken(ss.at[1], n_recv.at[1])

    @pl.when(not_first)
    def _():
        taken(sl.at[d], s_recv.at[d - 1])
        taken(ss.at[0], n_recv.at[0])

    @pl.when(not_last)
    def _():
        taken(sl.at[d + 2], s_recv.at[d + 1])
        taken(ss.at[2], n_recv.at[2])

    for a in (1, 0, 2):
        s = jnp.concatenate([sl[d + 2 - a], ss[2 - a]], axis=0).astype(F32)
        for cc, sc in ((1, s), (0, left(s)), (2, right(s))):
            for b, sb in ((1, sc), (0, down(sc)), (2, up(sc))):
                cm[pl.ds((a * 9 + b * 3 + cc) * O2, O2), :] = sb.astype(BF16)

    r_slot = rs.at[m]

    @pl.loop(0, 2)
    def _(n):
        zd = jnp.where(n == 0, 1 - zh, zh)
        lhs = jnp.concatenate(
            [kt[pl.ds(pl.multiple_of(i * 128 + zd * 64, 64), 64), :] for i in range(4)], axis=0
        )
        part = jnp.dot(lhs, cm[...], preferred_element_type=F32).astype(BF16)
        for i in range(4):
            og[pl.ds(pl.multiple_of(i * 128 + zd * 64, 64), 64), :] = part[i * 64 : i * 64 + 64]

        @pl.loop(0, 8)
        def _(i):
            far = (y + i // 2 + jnp.where(khalf == c, 2, 0)) % 4
            j = far * 4 + zd * 2 + i % 2
            to = 16 * c + j
            src = og.at[pl.ds(pl.multiple_of(j * CS, CS), CS)]

            @pl.when(to != k)
            def _():
                remote(src, r_slot, r_send, r_recv, (d, to)).start()

            @pl.when(to == k)
            def _():
                pltpu.make_async_copy(src, r_slot, r_recv).start()

    def spread_chans(odd_plane, forward):
        @pl.loop(0, 8, unroll=2)
        def _(j):
            p = (j // 2) * NL + 2 * (j % 2) + odd_plane
            taken(v2.at[p], v_recv.at[p])
            if forward:
                remote(v2.at[p], v2.at[p], f_send, v_recv.at[p], (d, sib)).start()
            v = v2[p].astype(F32)
            xc[p, pl.ds(0, 64), :] = right(v).astype(BF16)
            xc[p, pl.ds(64, 64), :] = v2[p]
            xc[p, pl.ds(128, 64), :] = left(v).astype(BF16)

    spread_chans(c, True)

    spread_chans(1 - c, False)

    @pl.loop(0, ND)
    def _(p):
        @pl.when(jnp.logical_or(p < d - 1, p > d + 1))
        def _():
            taken(sl.at[p + 1], s_recv.at[p])

    @pl.loop(0, ND, unroll=4)
    def _(p):
        v = sl[p + 1].astype(F32)
        slb[p + 1, pl.ds(0, CS), :] = down(v).astype(BF16)
        slb[p + 1, pl.ds(CS, CS), :] = sl[p + 1]
        slb[p + 1, pl.ds(2 * CS, CS), :] = up(v).astype(BF16)

    for p in range(0, ND, 4):
        lhs = jnp.concatenate(
            [slb[pl.ds(p + i, 3)].reshape(9 * CS, VOX) for i in range(4)], axis=1
        )
        rhs = jnp.concatenate([xc[p + i] for i in range(4)], axis=1)
        part = lax.dot_general(lhs, rhs, (((1,), (1,)), ((), ())), preferred_element_type=F32)
        acc[...] = part if p == 0 else acc[...] + part

    for a in range(3):
        for b in range(3):
            rows = acc[pl.ds(((2 - a) * 3 + b) * CS, CS), :]
            for cc in range(3):
                part = rows[:, cc * 64 : cc * 64 + 64]
                kg_ref[a * 9 + b * 3 + cc] = part

    taken(rs, r_recv)
    total = rs[0].astype(F32)
    for j in range(1, 16):
        total = total + rs[j].astype(F32)
    ig_ref[...] = total.T.astype(BF16)

    k_out.wait_send()
    for own, sem in ((self_a, a_send), (self_a, r_send)):
        @pl.when(own)
        def _():
            taken(xh.at[pl.ds(0, 15 * CS)], sem)

        @pl.when(jnp.logical_not(own))
        def _():
            taken(xh, sem)

    @pl.when(self_v)
    def _():
        taken(v2.at[pl.ds(0, 7)], v_send)

    @pl.when(jnp.logical_not(self_v))
    def _():
        taken(v2.at[pl.ds(0, 8)], v_send)

    taken(v2.at[pl.ds(0, 8)], f_send)
    taken(psend.at[1, 1], p_send.at[2])

    @pl.when(not_last)
    def _():
        for r in range(2):
            taken(psend.at[0, r], p_send.at[3 + r])
        taken(mine, n_send.at[2])

    @pl.when(not_first)
    def _():
        for r in range(2):
            taken(psend.at[2, r], p_send.at[5 + r])
        taken(mine, n_send.at[0])

    taken(mine, n_send.at[1])

    @pl.loop(1, ND)
    def _(n):
        taken(mine, s_send.at[n])


def local(volume, cotangent, kernel):
    in_hbm = pl.BlockSpec(memory_space=pltpu.HBM)
    in_vmem = pl.BlockSpec(memory_space=pltpu.VMEM)
    dma = pltpu.SemaphoreType.DMA
    ig, kg = pl.pallas_call(
        kernel_body,
        out_shape=(
            jax.ShapeDtypeStruct((VOX, CS), BF16),
            jax.ShapeDtypeStruct((TAPS, CS, 64), F32),
        ),
        in_specs=[in_hbm] * 3,
        out_specs=(in_vmem, in_vmem),
        scratch_shapes=[
            pltpu.VMEM((VOX, CS), BF16),
            pltpu.VMEM((VOX, CS), BF16),
            pltpu.VMEM((CS, VOX), BF16),
            pltpu.VMEM((HALF, VOX), BF16),
                    pltpu.VMEM((28, O2, HALF), BF16),
            pltpu.VMEM((HALF, TPAD), BF16),
            pltpu.VMEM((3, 2, CS, VOX), BF16),
            pltpu.VMEM((3, 2, CS, VOX), BF16),
            pltpu.VMEM((CS, VOX), F32),
            pltpu.VMEM((ND + 2, CS, VOX), BF16),
            pltpu.VMEM((3, CS, VOX), BF16),
            pltpu.VMEM((TPAD, VOX), BF16),
            pltpu.VMEM((HALF, VOX), BF16),
            pltpu.VMEM((16, CS, VOX), BF16),
            pltpu.VMEM((ND, 64, VOX), BF16),
            pltpu.VMEM((ND, 192, VOX), BF16),
            pltpu.VMEM((ND + 2, 3 * CS, VOX), BF16),
            pltpu.VMEM((9 * CS, 192), F32),
            dma((3,)), dma, dma, dma, dma, dma((7,)), dma((3, 2)), dma((ND,)), dma((ND,)),
            dma((3,)), dma((3,)), dma, dma((ND,)), dma, dma, dma,
        ],
        compiler_params=pltpu.CompilerParams(
            collective_id=0, has_side_effects=True, vmem_limit_bytes=48 * 2**20
        ),
        cost_estimate=pl.CostEstimate(
            flops=3 * 453_000_000, bytes_accessed=6_000_000, transcendentals=8192
        ),
    )(
        pltpu.with_memory_space_constraint(volume.reshape(VOX, CS), pltpu.HBM),
        pltpu.with_memory_space_constraint(cotangent.reshape(VOX, CS), pltpu.HBM),
        pltpu.with_memory_space_constraint(jnp.transpose(kernel, (1, 0, 2)), pltpu.HBM),
    )
    ig, kg = pl.pallas_call(
        finish,
        out_shape=(
            jax.ShapeDtypeStruct((VOX, CS), BF16),
            jax.ShapeDtypeStruct((TAPS, CS, 64), F32),
        ),
        in_specs=[pl.BlockSpec(memory_space=pl.ANY)] * 2,
        out_specs=(pl.BlockSpec(memory_space=pl.ANY),) * 2,
        scratch_shapes=[dma((2,))],
    )(*(pltpu.with_memory_space_constraint(v, pltpu.VMEM) for v in (ig, kg)))
    input_grad = ig.reshape(1, SIDE, SIDE, CS)
    kernel_grad = jnp.transpose(kg, (1, 0, 2))[None]
    return (input_grad, kernel_grad)


def solution(mesh):
    return jax.shard_map(
        local,
        mesh=mesh,
        in_specs=(
            P("depth", None, None, "chan"),
            P("depth", None, None, "chan"),
            P("chan", None, None),
        ),
        out_specs=(P("depth", None, None, "chan"), P("chan", None, None, "depth")),
        check_vma=False,
    )
```

```python
import functools

import jax
import jax.numpy as jnp
from jax import lax
from jax.experimental import pallas as pl
from jax.experimental.pallas import tpu as pltpu
from jax.sharding import PartitionSpec as P

MESH = pl.DeviceIdType.MESH
F32, BF16 = jnp.float32, jnp.bfloat16
ND, NX, NL, NZ, NK = 16, 4, 4, 8, 32
CS, SIDE, VOX, CH = 32, 16, 256, 1024
HALF, TAPS, O2 = 512, 27, 64
TROWS, TPAD = TAPS * O2, 28 * O2


def finish(ig_ref, kg_ref, ig_out, kg_out, sem):
    a = pltpu.make_async_copy(ig_ref, ig_out, sem.at[0])
    b = pltpu.make_async_copy(kg_ref, kg_out, sem.at[1])
    b.start()
    a.start()
    a.wait()
    b.wait()


def kernel_body(
    vol_hbm, cot_hbm, k_hbm, ig_ref, kg_ref,
    vin, cin, xt, xh, k2, kt, psend, prec, held, sl, ss, cm, og, rs, v2, xc, slb, acc,
    in_sem, k_send, k_recv, a_send, a_recv, p_send, p_recv, s_send, s_recv, n_send, n_recv,
    v_send, v_recv, f_send, r_send, r_recv,
):
    d, k = lax.axis_index("depth"), lax.axis_index("chan")
    x, zl = d // NL, d % NL
    y, zh, c, m = k // 4, (k // 2) % 2, k % 2, k // 2
    z, sib = zh * NL + zl, k + 1 - 2 * c
    khalf = k // 16
    self_a = khalf == c
    self_v = jnp.logical_and(zl % 2 == c, x // 2 == c)

    def remote(src, dst, ssem, rsem, dev):
        return pltpu.make_async_remote_copy(
            src_ref=src, dst_ref=dst, send_sem=ssem, recv_sem=rsem, device_id=dev,
            device_id_type=MESH,
        )

    def taken(ref, sem):
        pltpu.make_async_copy(ref, ref, sem).wait()

    vol_in = pltpu.make_async_copy(vol_hbm, vin, in_sem.at[0])
    cot_in = pltpu.make_async_copy(cot_hbm, cin, in_sem.at[1])
    k_in = pltpu.make_async_copy(
        k_hbm.at[:, :, pl.ds(pl.multiple_of(c * HALF, HALF), HALF)],
        k2.at[pl.ds(0, TAPS), pl.ds(0, CS)], in_sem.at[2],
    )
    vol_in.start()
    cot_in.start()
    k_in.start()

    bar = pltpu.get_barrier_semaphore()

    def greet(dd, kk):
        pl.semaphore_signal(bar, inc=1, device_id=(dd, kk), device_id_type=MESH)

    def far_first(j):
        i = j % 8
        dy = 4 + jnp.where(i % 2 == 1, -((i + 1) // 2), i // 2)
        yy = (y + dy) % 8
        return yy, yy * 2 + jnp.where(j < 8, 1 - zh, zh)

    @pl.loop(0, 16)
    def _(j):
        yy, mm = far_first(j)
        mine = 2 * mm + khalf

        @pl.when(mine != k)
        def _():
            greet(d, mine)

        @pl.when(jnp.logical_and(yy // 4 == c, mine + 1 - 2 * khalf != k))
        def _():
            greet(d, mine + 1 - 2 * khalf)

    @pl.loop(1, 4)
    def _(j):
        greet((x + j) % NX * NL + zl, k)
        greet(x * NL + (zl + j) % NL, k)

    for kk in (k, sib):
        greet((d + 1) % ND, kk)
        greet((d + ND - 1) % ND, kk)

    odd = (z + c) % 2

    @pl.loop(0, 8)
    def _(j):
        xs, t = j // 2, j % 2
        step = jnp.where(odd == 1, 2 * t - 1, t * (2 - 4 * (xs % 2)))
        zs = (z - step + NZ) % NZ
        dd, kk = xs * NL + zs % NL, (y * 2 + zs // NL) * 2 + x // 2

        @pl.when(jnp.logical_or(dd != d, kk != k))
        def _():
            greet(dd, kk)

    vol_in.wait()
    xt[...] = vin[...].astype(F32).T.astype(BF16)

    zero = jnp.zeros((CS, VOX), BF16)
    slb[0] = jnp.zeros((3 * CS, VOX), BF16)
    slb[ND + 1] = jnp.zeros((3 * CS, VOX), BF16)
    sl[0] = zero
    sl[ND + 1] = zero
    cm[pl.ds(TROWS, O2), :] = jnp.zeros((O2, VOX), BF16)
    k2[TAPS] = jnp.zeros((O2, HALF), BF16)

    @pl.when(d == 0)
    def _():
        prec[0] = jnp.zeros((2, CS, VOX), BF16)
        ss[0] = zero

    @pl.when(d == ND - 1)
    def _():
        prec[2] = jnp.zeros((2, CS, VOX), BF16)
        ss[2] = zero

    sa, sv = self_a.astype(jnp.int32), self_v.astype(jnp.int32)
    pl.semaphore_wait(bar, 24 - sa + 6 + 4 + 8 - sv)

    a_slot = xh.at[pl.ds(pl.multiple_of((k % 16) * CS, CS), CS)]

    @pl.loop(0, 16)
    def _(j):
        to = 2 * far_first(j)[1] + khalf

        @pl.when(to != k)
        def _():
            remote(xt, a_slot, a_send, a_recv.at[zh], (d, to)).start()

        @pl.when(to == k)
        def _():
            pltpu.make_async_copy(xt, a_slot, a_recv.at[zh]).start()

    k_out = remote(
        k_hbm.at[:, :, pl.ds(pl.multiple_of((1 - c) * HALF, HALF), HALF)],
        k2.at[pl.ds(0, TAPS), pl.ds(CS, CS)], k_send, k_recv, (d, sib),
    )
    k_out.start()

    k_in.wait()
    k_out.wait_recv()
    for p in range(14):
        kt[:, pl.ds(p * 128, 128)] = k2[pl.ds(2 * p, 2)].reshape(128, HALF).T

    lane = lax.broadcasted_iota(jnp.int32, (1, VOX), 1)
    hh, ww = lane // SIDE, lane % SIDE
    h_lo, h_hi = hh >= 1, hh <= SIDE - 2
    w_lo, w_hi = ww >= 1, ww <= SIDE - 2

    def moved(v, step, keep):
        return jnp.where(keep, pltpu.roll(v, step % VOX, 1), 0.0)

    def up(v):
        return moved(v, SIDE, h_lo)

    def down(v):
        return moved(v, -SIDE, h_hi)

    def right(v):
        return moved(v, 1, w_lo)

    def left(v):
        return moved(v, -1, w_hi)

    def spread_out(other):
      @pl.loop(0, 4)
      def _(j):
        xd, t = 2 * c + j % 2, j // 2
        even = (z + zh + other) % 2 == 0
        step = jnp.where(even, (1 - t) * (2 - 4 * (x % 2)), 2 * t - 1)
        zd = (z + step + NZ) % NZ
        dd, kk = xd * NL + zd % NL, (y * 2 + zd // NL) * 2 + zl % 2
        src = xh.at[pl.ds(pl.multiple_of(((j % 2) * NL + zd % NL) * 64, 64), 64)]
        own = jnp.logical_and(dd == d, kk == k)

        @pl.when(jnp.logical_not(own))
        def _():
            remote(src, v2.at[d], v_send, v_recv.at[d], (dd, kk)).start()

        @pl.when(own)
        def _():
            pltpu.make_async_copy(src, v2.at[d], v_recv.at[d]).start()

    taken(xh.at[pl.ds(0, 8 * CS)], a_recv.at[zh])
    spread_out(0)
    taken(xh.at[pl.ds(0, 8 * CS)], a_recv.at[1 - zh])
    xv = xh[...]

    for a in (0, 2, 1):
        yv = jnp.dot(k2[pl.ds(a * 9, 9)].reshape(9 * O2, HALF), xv, preferred_element_type=F32)

        def tap(b, cc):
            at = (b * 3 + cc) * O2
            return yv[at : at + O2, :]

        cols = [tap(1, cc) + up(tap(0, cc)) + down(tap(2, cc)) for cc in range(3)]
        tot = cols[1] + right(cols[0]) + left(cols[2])
        if a == 1:
            held[...] = tot[:CS]
            psend[a, 1] = tot[CS:].astype(BF16)
            remote(psend.at[1, 1], prec.at[1, c], p_send.at[2], p_recv.at[1, c], (d, sib)).start()
        else:
            psend[a, 0] = tot[:CS].astype(BF16)
            psend[a, 1] = tot[CS:].astype(BF16)
            i = 0 if a == 0 else 1
            there = d + 1 - a

            @pl.when(jnp.logical_and(there >= 0, there < ND))
            def _():
                for r, kk in ((0, k), (1, sib)):
                    remote(
                        psend.at[a, r], prec.at[a, c], p_send.at[3 + 2 * i + r], p_recv.at[a, c],
                        (there, kk),
                    ).start()

    spread_out(1)

    cot_in.wait()
    cot_t = cin[...].astype(F32).T
    not_first, not_last = d >= 1, d <= ND - 2
    taken(prec.at[1, 1 - c], p_recv.at[1, 1 - c])

    @pl.when(not_first)
    def _():
        taken(prec.at[0, 0], p_recv.at[0, 0])
        taken(prec.at[0, 1], p_recv.at[0, 1])

    @pl.when(not_last)
    def _():
        taken(prec.at[2, 0], p_recv.at[2, 0])
        taken(prec.at[2, 1], p_recv.at[2, 1])

    got = [prec[1, 1 - c], prec[0, 0], prec[0, 1], prec[2, 0], prec[2, 1]]
    pre = held[...] + sum(v.astype(F32) for v in got)
    sig = 1.0 / (1.0 + jnp.exp(-pre))
    sl[d + 1] = (cot_t * sig * (1.0 + pre * (1.0 - sig))).astype(BF16)

    mine = sl.at[d + 1]

    def slope_out(plane, to, i):
        at = sl.at[plane + 1]
        return remote(at, at, s_send.at[i], s_recv.at[plane], (to, k))

    far_up, far_down = jnp.logical_and(zl == 3, not_last), jnp.logical_and(zl == 0, not_first)

    def own_copies(act):
        @pl.when(far_up)
        def _():
            act(d, d + 1, 8)

        @pl.when(far_down)
        def _():
            act(d, d - 1, 9)

        @pl.loop(0, NL)
        def _(t):
            @pl.when(t != zl)
            def _():
                act(d, x * NL + t, t)

    def own_along_x(act):
        @pl.loop(0, NX)
        def _(t):
            @pl.when(t != x)
            def _():
                act(d, t * NL + zl, 4 + t)

    def passed_on(act, first):
        @pl.loop(0, NL)
        def _(zs):
            p = x * NL + zs

            @pl.when(zs != zl)
            def _():
                first(p)

                @pl.loop(0, NX)
                def _(t):
                    to = t * NL + zl
                    near = jnp.logical_or(to == p + 1, to == p - 1)

                    @pl.when(jnp.logical_and(t != x, jnp.logical_not(near)))
                    def _():
                        act(p, to, 16 + zs * NX + t)

    def send(plane, to, i):
        slope_out(plane, to, i).start()

    def sent(plane, to, i):
        taken(mine, s_send.at[i])

    own_copies(send)
    remote(mine, ss.at[1], n_send.at[1], n_recv.at[1], (d, sib)).start()

    @pl.when(not_first)
    def _():
        remote(mine, ss.at[2], n_send.at[0], n_recv.at[2], (d - 1, sib)).start()

    @pl.when(not_last)
    def _():
        remote(mine, ss.at[0], n_send.at[2], n_recv.at[0], (d + 1, sib)).start()

    own_along_x(send)

    def columns(a):
        s = jnp.concatenate([sl[d + 2 - a], ss[2 - a]], axis=0).astype(F32)
        for cc, sc in ((1, s), (0, left(s)), (2, right(s))):
            for b, sb in ((1, sc), (0, down(sc)), (2, up(sc))):
                cm[pl.ds((a * 9 + b * 3 + cc) * O2, O2), :] = sb.astype(BF16)

    taken(ss.at[1], n_recv.at[1])
    columns(1)

    @pl.when(not_first)
    def _():
        taken(sl.at[d], s_recv.at[d - 1])
        taken(ss.at[0], n_recv.at[0])

    @pl.when(not_last)
    def _():
        taken(sl.at[d + 2], s_recv.at[d + 1])
        taken(ss.at[2], n_recv.at[2])

    columns(0)
    columns(2)

    r_slot = rs.at[m]

    @pl.loop(0, 2)
    def _(n):
        zd = jnp.where(n == 0, 1 - zh, zh)
        lhs = jnp.concatenate(
            [kt[pl.ds(pl.multiple_of(i * 128 + zd * 64, 64), 64), :] for i in range(4)], axis=0
        )
        part = jnp.dot(lhs, cm[...], preferred_element_type=F32).astype(BF16)
        for i in range(4):
            og[pl.ds(pl.multiple_of(i * 128 + zd * 64, 64), 64), :] = part[i * 64 : i * 64 + 64]

        @pl.loop(0, 8)
        def _(i):
            far = (y + i // 2 + jnp.where(khalf == c, 2, 0)) % 4
            j = far * 4 + zd * 2 + i % 2
            to = 16 * c + j
            src = og.at[pl.ds(pl.multiple_of(j * CS, CS), CS)]

            @pl.when(to != k)
            def _():
                remote(src, r_slot, r_send, r_recv, (d, to)).start()

            @pl.when(to == k)
            def _():
                pltpu.make_async_copy(src, r_slot, r_recv).start()

    def arrived(p):
        @pl.when(jnp.logical_or(p < d - 1, p > d + 1))
        def _():
            taken(sl.at[p + 1], s_recv.at[p])

    passed_on(send, arrived)

    def spread_chans(odd_plane, forward):
        @pl.loop(0, 8, unroll=2)
        def _(j):
            p = (j // 2) * NL + 2 * (j % 2) + odd_plane
            taken(v2.at[p], v_recv.at[p])
            if forward:
                remote(v2.at[p], v2.at[p], f_send, v_recv.at[p], (d, sib)).start()
            v = v2[p].astype(F32)
            xc[p, pl.ds(0, 64), :] = right(v).astype(BF16)
            xc[p, pl.ds(64, 64), :] = v2[p]
            xc[p, pl.ds(128, 64), :] = left(v).astype(BF16)

    spread_chans(c, True)

    spread_chans(1 - c, False)

    @pl.loop(0, ND)
    def _(p):
        @pl.when(p // NL != x)
        def _():
            arrived(p)

    @pl.loop(0, ND, unroll=4)
    def _(p):
        v = sl[p + 1].astype(F32)
        slb[p + 1, pl.ds(0, CS), :] = down(v).astype(BF16)
        slb[p + 1, pl.ds(CS, CS), :] = sl[p + 1]
        slb[p + 1, pl.ds(2 * CS, CS), :] = up(v).astype(BF16)

    for p in range(0, ND, 4):
        lhs = jnp.concatenate(
            [slb[pl.ds(p + i, 3)].reshape(9 * CS, VOX) for i in range(4)], axis=1
        )
        rhs = jnp.concatenate([xc[p + i] for i in range(4)], axis=1)
        part = lax.dot_general(lhs, rhs, (((1,), (1,)), ((), ())), preferred_element_type=F32)
        acc[...] = part if p == 0 else acc[...] + part

    for a in range(3):
        for b in range(3):
            rows = acc[pl.ds(((2 - a) * 3 + b) * CS, CS), :]
            for cc in range(3):
                part = rows[:, cc * 64 : cc * 64 + 64]
                kg_ref[a * 9 + b * 3 + cc] = part

    k_out.wait_send()
    for own, sem in ((self_a, a_send), (self_a, r_send)):
        @pl.when(own)
        def _():
            taken(xh.at[pl.ds(0, 15 * CS)], sem)

        @pl.when(jnp.logical_not(own))
        def _():
            taken(xh, sem)

    @pl.when(self_v)
    def _():
        taken(v2.at[pl.ds(0, 7)], v_send)

    @pl.when(jnp.logical_not(self_v))
    def _():
        taken(v2.at[pl.ds(0, 8)], v_send)

    taken(v2.at[pl.ds(0, 8)], f_send)
    taken(psend.at[1, 1], p_send.at[2])

    @pl.when(not_last)
    def _():
        for r in range(2):
            taken(psend.at[0, r], p_send.at[3 + r])
        taken(mine, n_send.at[2])

    @pl.when(not_first)
    def _():
        for r in range(2):
            taken(psend.at[2, r], p_send.at[5 + r])
        taken(mine, n_send.at[0])

    taken(mine, n_send.at[1])

    own_copies(sent)
    own_along_x(sent)
    passed_on(sent, lambda p: None)

    taken(rs, r_recv)
    total = rs[0].astype(F32)
    for j in range(1, 16):
        total = total + rs[j].astype(F32)
    ig_ref[...] = total.T.astype(BF16)


def local(volume, cotangent, kernel):
    in_hbm = pl.BlockSpec(memory_space=pltpu.HBM)
    in_vmem = pl.BlockSpec(memory_space=pltpu.VMEM)
    dma = pltpu.SemaphoreType.DMA
    ig, kg = pl.pallas_call(
        kernel_body,
        out_shape=(
            jax.ShapeDtypeStruct((VOX, CS), BF16),
            jax.ShapeDtypeStruct((TAPS, CS, 64), F32),
        ),
        in_specs=[in_hbm] * 3,
        out_specs=(in_vmem, in_vmem),
        scratch_shapes=[
            pltpu.VMEM((VOX, CS), BF16),
            pltpu.VMEM((VOX, CS), BF16),
            pltpu.VMEM((CS, VOX), BF16),
            pltpu.VMEM((HALF, VOX), BF16),
                    pltpu.VMEM((28, O2, HALF), BF16),
            pltpu.VMEM((HALF, TPAD), BF16),
            pltpu.VMEM((3, 2, CS, VOX), BF16),
            pltpu.VMEM((3, 2, CS, VOX), BF16),
            pltpu.VMEM((CS, VOX), F32),
            pltpu.VMEM((ND + 2, CS, VOX), BF16),
            pltpu.VMEM((3, CS, VOX), BF16),
            pltpu.VMEM((TPAD, VOX), BF16),
            pltpu.VMEM((HALF, VOX), BF16),
            pltpu.VMEM((16, CS, VOX), BF16),
            pltpu.VMEM((ND, 64, VOX), BF16),
            pltpu.VMEM((ND, 192, VOX), BF16),
            pltpu.VMEM((ND + 2, 3 * CS, VOX), BF16),
            pltpu.VMEM((9 * CS, 192), F32),
            dma((3,)), dma, dma, dma, dma((2,)), dma((7,)), dma((3, 2)), dma((32,)), dma((ND,)),
            dma((3,)), dma((3,)), dma, dma((ND,)), dma, dma, dma,
        ],
        compiler_params=pltpu.CompilerParams(
            collective_id=0, has_side_effects=True, vmem_limit_bytes=48 * 2**20
        ),
        cost_estimate=pl.CostEstimate(
            flops=3 * 453_000_000, bytes_accessed=6_000_000, transcendentals=8192
        ),
    )(
        pltpu.with_memory_space_constraint(volume.reshape(VOX, CS), pltpu.HBM),
        pltpu.with_memory_space_constraint(cotangent.reshape(VOX, CS), pltpu.HBM),
        pltpu.with_memory_space_constraint(jnp.transpose(kernel, (1, 0, 2)), pltpu.HBM),
    )
    ig, kg = pl.pallas_call(
        finish,
        out_shape=(
            jax.ShapeDtypeStruct((VOX, CS), BF16),
            jax.ShapeDtypeStruct((TAPS, CS, 64), F32),
        ),
        in_specs=[pl.BlockSpec(memory_space=pl.ANY)] * 2,
        out_specs=(pl.BlockSpec(memory_space=pl.ANY),) * 2,
        scratch_shapes=[dma((2,))],
    )(*(pltpu.with_memory_space_constraint(v, pltpu.VMEM) for v in (ig, kg)))
    input_grad = ig.reshape(1, SIDE, SIDE, CS)
    kernel_grad = jnp.transpose(kg, (1, 0, 2))[None]
    return (input_grad, kernel_grad)


def solution(mesh):
    return jax.shard_map(
        local,
        mesh=mesh,
        in_specs=(
            P("depth", None, None, "chan"),
            P("depth", None, None, "chan"),
            P("chan", None, None),
        ),
        out_specs=(P("depth", None, None, "chan"), P("chan", None, None, "depth")),
        check_vma=False,
    )
```

```python
import functools

import jax
import jax.numpy as jnp
from jax import lax
from jax.experimental import pallas as pl
from jax.experimental.pallas import tpu as pltpu
from jax.sharding import PartitionSpec as P

MESH = pl.DeviceIdType.MESH
F32, BF16 = jnp.float32, jnp.bfloat16
ND, NX, NL, NZ, NK = 16, 4, 4, 8, 32
CS, SIDE, VOX, CH = 32, 16, 256, 1024
HALF, TAPS, O2 = 512, 27, 64
TROWS, TPAD = TAPS * O2, 28 * O2


def finish(ig_ref, kg_ref, ig_out, kg_out, sem):
    a = pltpu.make_async_copy(ig_ref, ig_out, sem.at[0])
    b = pltpu.make_async_copy(kg_ref, kg_out, sem.at[1])
    b.start()
    a.start()
    a.wait()
    b.wait()


def kernel_body(
    vol_hbm, cot_hbm, k_hbm, ig_ref, kg_ref,
    vin, cin, xt, xh, k2, kt, psend, prec, held, sl, ss, cm, og, rs, v2, xc, slb, acc,
    in_sem, k_send, k_recv, a_send, a_recv, p_send, p_recv, s_send, s_recv, n_send, n_recv,
    v_send, v_recv, f_send, r_send, r_recv,
):
    d, k = lax.axis_index("depth"), lax.axis_index("chan")
    x, zl = d // NL, d % NL
    y, zh, c, m = k // 4, (k // 2) % 2, k % 2, k // 2
    z, sib = zh * NL + zl, k + 1 - 2 * c
    khalf = k // 16
    self_a = khalf == c
    self_v = jnp.logical_and(zl % 2 == c, x // 2 == c)

    def remote(src, dst, ssem, rsem, dev):
        return pltpu.make_async_remote_copy(
            src_ref=src, dst_ref=dst, send_sem=ssem, recv_sem=rsem, device_id=dev,
            device_id_type=MESH,
        )

    def taken(ref, sem):
        pltpu.make_async_copy(ref, ref, sem).wait()

    vol_in = pltpu.make_async_copy(vol_hbm, vin, in_sem.at[0])
    cot_in = pltpu.make_async_copy(cot_hbm, cin, in_sem.at[1])
    k_in = pltpu.make_async_copy(
        k_hbm.at[:, :, pl.ds(pl.multiple_of(c * HALF, HALF), HALF)],
        k2.at[pl.ds(0, TAPS), pl.ds(0, CS)], in_sem.at[2],
    )
    vol_in.start()
    cot_in.start()
    k_in.start()

    bar = pltpu.get_barrier_semaphore()

    def greet(dd, kk):
        pl.semaphore_signal(bar, inc=1, device_id=(dd, kk), device_id_type=MESH)

    def far_first(j):
        i = j % 8
        dy = 4 + jnp.where(i % 2 == 1, -((i + 1) // 2), i // 2)
        yy = (y + dy) % 8
        return yy, yy * 2 + jnp.where(j < 8, 1 - zh, zh)

    @pl.loop(0, 16)
    def _(j):
        yy, mm = far_first(j)
        mine = 2 * mm + khalf

        @pl.when(mine != k)
        def _():
            greet(d, mine)

        @pl.when(jnp.logical_and(yy // 4 == c, mine + 1 - 2 * khalf != k))
        def _():
            greet(d, mine + 1 - 2 * khalf)

    @pl.loop(1, 4)
    def _(j):
        greet((x + j) % NX * NL + zl, k)
        greet(x * NL + (zl + j) % NL, k)

    for kk in (k, sib):
        greet((d + 1) % ND, kk)
        greet((d + ND - 1) % ND, kk)

    odd = (z + c) % 2

    @pl.loop(0, 8)
    def _(j):
        xs, t = j // 2, j % 2
        step = jnp.where(odd == 1, 2 * t - 1, t * (2 - 4 * (xs % 2)))
        zs = (z - step + NZ) % NZ
        dd, kk = xs * NL + zs % NL, (y * 2 + zs // NL) * 2 + x // 2

        @pl.when(jnp.logical_or(dd != d, kk != k))
        def _():
            greet(dd, kk)

    vol_in.wait()
    xt[...] = vin[...].astype(F32).T.astype(BF16)

    zero = jnp.zeros((CS, VOX), BF16)
    slb[0] = jnp.zeros((3 * CS, VOX), BF16)
    slb[ND + 1] = jnp.zeros((3 * CS, VOX), BF16)
    sl[0] = zero
    sl[ND + 1] = zero
    cm[pl.ds(TROWS, O2), :] = jnp.zeros((O2, VOX), BF16)
    k2[TAPS] = jnp.zeros((O2, HALF), BF16)

    @pl.when(d == 0)
    def _():
        prec[0] = jnp.zeros((2, CS, VOX), BF16)
        ss[0] = zero

    @pl.when(d == ND - 1)
    def _():
        prec[2] = jnp.zeros((2, CS, VOX), BF16)
        ss[2] = zero

    sa, sv = self_a.astype(jnp.int32), self_v.astype(jnp.int32)
    pl.semaphore_wait(bar, 24 - sa + 6 + 4 + 8 - sv)

    a_slot = xh.at[pl.ds(pl.multiple_of((k % 16) * CS, CS), CS)]

    @pl.loop(0, 16)
    def _(j):
        to = 2 * far_first(j)[1] + khalf

        @pl.when(to != k)
        def _():
            remote(xt, a_slot, a_send, a_recv.at[zh], (d, to)).start()

        @pl.when(to == k)
        def _():
            pltpu.make_async_copy(xt, a_slot, a_recv.at[zh]).start()

    k_out = remote(
        k_hbm.at[:, :, pl.ds(pl.multiple_of((1 - c) * HALF, HALF), HALF)],
        k2.at[pl.ds(0, TAPS), pl.ds(CS, CS)], k_send, k_recv, (d, sib),
    )
    k_out.start()

    k_in.wait()
    k_out.wait_recv()
    for p in range(14):
        kt[:, pl.ds(p * 128, 128)] = k2[pl.ds(2 * p, 2)].reshape(128, HALF).T

    lane = lax.broadcasted_iota(jnp.int32, (1, VOX), 1)
    hh, ww = lane // SIDE, lane % SIDE
    h_lo, h_hi = hh >= 1, hh <= SIDE - 2
    w_lo, w_hi = ww >= 1, ww <= SIDE - 2

    def moved(v, step, keep):
        return jnp.where(keep, pltpu.roll(v, step % VOX, 1), 0.0)

    def up(v):
        return moved(v, SIDE, h_lo)

    def down(v):
        return moved(v, -SIDE, h_hi)

    def right(v):
        return moved(v, 1, w_lo)

    def left(v):
        return moved(v, -1, w_hi)

    def spread_out(other):
      @pl.loop(0, 4)
      def _(j):
        xd, t = 2 * c + j % 2, j // 2
        even = (z + zh + other) % 2 == 0
        step = jnp.where(even, (1 - t) * (2 - 4 * (x % 2)), 2 * t - 1)
        zd = (z + step + NZ) % NZ
        dd, kk = xd * NL + zd % NL, (y * 2 + zd // NL) * 2 + zl % 2
        src = xh.at[pl.ds(pl.multiple_of(((j % 2) * NL + zd % NL) * 64, 64), 64)]
        own = jnp.logical_and(dd == d, kk == k)

        @pl.when(jnp.logical_not(own))
        def _():
            remote(src, v2.at[d], v_send, v_recv.at[d], (dd, kk)).start()

        @pl.when(own)
        def _():
            pltpu.make_async_copy(src, v2.at[d], v_recv.at[d]).start()

    taken(xh.at[pl.ds(0, 8 * CS)], a_recv.at[zh])
    spread_out(0)
    taken(xh.at[pl.ds(0, 8 * CS)], a_recv.at[1 - zh])
    xv = xh[...]

    for a in (0, 2, 1):
        yv = jnp.dot(k2[pl.ds(a * 9, 9)].reshape(9 * O2, HALF), xv, preferred_element_type=F32)

        def tap(b, cc):
            at = (b * 3 + cc) * O2
            return yv[at : at + O2, :]

        cols = [tap(1, cc) + up(tap(0, cc)) + down(tap(2, cc)) for cc in range(3)]
        tot = cols[1] + right(cols[0]) + left(cols[2])
        if a == 1:
            held[...] = tot[:CS]
            psend[a, 1] = tot[CS:].astype(BF16)
            remote(psend.at[1, 1], prec.at[1, c], p_send.at[2], p_recv.at[1, c], (d, sib)).start()
        else:
            psend[a, 0] = tot[:CS].astype(BF16)
            psend[a, 1] = tot[CS:].astype(BF16)
            i = 0 if a == 0 else 1
            there = d + 1 - a

            @pl.when(jnp.logical_and(there >= 0, there < ND))
            def _():
                for r, kk in ((0, k), (1, sib)):
                    remote(
                        psend.at[a, r], prec.at[a, c], p_send.at[3 + 2 * i + r], p_recv.at[a, c],
                        (there, kk),
                    ).start()

    spread_out(1)

    cot_in.wait()
    cot_t = cin[...].astype(F32).T
    not_first, not_last = d >= 1, d <= ND - 2
    taken(prec.at[1, 1 - c], p_recv.at[1, 1 - c])

    @pl.when(not_first)
    def _():
        taken(prec.at[0, 0], p_recv.at[0, 0])
        taken(prec.at[0, 1], p_recv.at[0, 1])

    @pl.when(not_last)
    def _():
        taken(prec.at[2, 0], p_recv.at[2, 0])
        taken(prec.at[2, 1], p_recv.at[2, 1])

    got = [prec[1, 1 - c], prec[0, 0], prec[0, 1], prec[2, 0], prec[2, 1]]
    pre = held[...] + sum(v.astype(F32) for v in got)
    sig = 1.0 / (1.0 + jnp.exp(-pre))
    sl[d + 1] = (cot_t * sig * (1.0 + pre * (1.0 - sig))).astype(BF16)

    mine = sl.at[d + 1]

    def slope_out(plane, to, i):
        at = sl.at[plane + 1]
        return remote(at, at, s_send.at[i], s_recv.at[plane], (to, k))

    far_up, far_down = jnp.logical_and(zl == 3, not_last), jnp.logical_and(zl == 0, not_first)

    def own_copies(act):
        @pl.when(far_up)
        def _():
            act(d, d + 1, 8)

        @pl.when(far_down)
        def _():
            act(d, d - 1, 9)

        @pl.when(zl < NL - 1)
        def _():
            act(d, d + 1, zl + 1)

        @pl.when(zl > 0)
        def _():
            act(d, d - 1, zl - 1)

    def own_along(act):
        @pl.loop(0, NL)
        def _(t):
            @pl.when(jnp.logical_or(t < zl - 1, t > zl + 1))
            def _():
                act(d, x * NL + t, t)

        @pl.loop(0, NX)
        def _(t):
            @pl.when(t != x)
            def _():
                act(d, t * NL + zl, 4 + t)

    def passed_on(act, first):
        @pl.loop(0, NL)
        def _(zs):
            p = x * NL + zs

            @pl.when(zs != zl)
            def _():
                first(p)

                @pl.loop(0, NX)
                def _(t):
                    to = t * NL + zl
                    near = jnp.logical_or(to == p + 1, to == p - 1)

                    @pl.when(jnp.logical_and(t != x, jnp.logical_not(near)))
                    def _():
                        act(p, to, 16 + zs * NX + t)

    def send(plane, to, i):
        slope_out(plane, to, i).start()

    def sent(plane, to, i):
        taken(mine, s_send.at[i])

    own_copies(send)
    remote(mine, ss.at[1], n_send.at[1], n_recv.at[1], (d, sib)).start()

    @pl.when(not_first)
    def _():
        remote(mine, ss.at[2], n_send.at[0], n_recv.at[2], (d - 1, sib)).start()

    @pl.when(not_last)
    def _():
        remote(mine, ss.at[0], n_send.at[2], n_recv.at[0], (d + 1, sib)).start()

    own_along(send)

    def columns(a):
        s = jnp.concatenate([sl[d + 2 - a], ss[2 - a]], axis=0).astype(F32)
        for cc, sc in ((1, s), (0, left(s)), (2, right(s))):
            for b, sb in ((1, sc), (0, down(sc)), (2, up(sc))):
                cm[pl.ds((a * 9 + b * 3 + cc) * O2, O2), :] = sb.astype(BF16)

    taken(ss.at[1], n_recv.at[1])
    columns(1)

    @pl.when(not_first)
    def _():
        taken(sl.at[d], s_recv.at[d - 1])
        taken(ss.at[0], n_recv.at[0])

    @pl.when(not_last)
    def _():
        taken(sl.at[d + 2], s_recv.at[d + 1])
        taken(ss.at[2], n_recv.at[2])

    columns(0)
    columns(2)

    r_slot = rs.at[m]

    @pl.loop(0, 2)
    def _(n):
        zd = jnp.where(n == 0, 1 - zh, zh)
        lhs = jnp.concatenate(
            [kt[pl.ds(pl.multiple_of(i * 128 + zd * 64, 64), 64), :] for i in range(4)], axis=0
        )
        part = jnp.dot(lhs, cm[...], preferred_element_type=F32).astype(BF16)
        for i in range(4):
            og[pl.ds(pl.multiple_of(i * 128 + zd * 64, 64), 64), :] = part[i * 64 : i * 64 + 64]

        @pl.loop(0, 8)
        def _(i):
            far = (y + i // 2 + jnp.where(khalf == c, 2, 0)) % 4
            j = far * 4 + zd * 2 + i % 2
            to = 16 * c + j
            src = og.at[pl.ds(pl.multiple_of(j * CS, CS), CS)]

            @pl.when(to != k)
            def _():
                remote(src, r_slot, r_send, r_recv, (d, to)).start()

            @pl.when(to == k)
            def _():
                pltpu.make_async_copy(src, r_slot, r_recv).start()

    def arrived(p):
        @pl.when(jnp.logical_or(p < d - 1, p > d + 1))
        def _():
            taken(sl.at[p + 1], s_recv.at[p])

    passed_on(send, arrived)

    def spread_chans(odd_plane, forward):
        @pl.loop(0, 8, unroll=2)
        def _(j):
            p = (j // 2) * NL + 2 * (j % 2) + odd_plane
            taken(v2.at[p], v_recv.at[p])
            if forward:
                remote(v2.at[p], v2.at[p], f_send, v_recv.at[p], (d, sib)).start()
            v = v2[p].astype(F32)
            xc[p, pl.ds(0, 64), :] = right(v).astype(BF16)
            xc[p, pl.ds(64, 64), :] = v2[p]
            xc[p, pl.ds(128, 64), :] = left(v).astype(BF16)

    spread_chans(c, True)

    spread_chans(1 - c, False)

    @pl.loop(0, ND)
    def _(p):
        @pl.when(p // NL != x)
        def _():
            arrived(p)

    @pl.loop(0, ND, unroll=4)
    def _(p):
        v = sl[p + 1].astype(F32)
        slb[p + 1, pl.ds(0, CS), :] = down(v).astype(BF16)
        slb[p + 1, pl.ds(CS, CS), :] = sl[p + 1]
        slb[p + 1, pl.ds(2 * CS, CS), :] = up(v).astype(BF16)

    for p in range(0, ND, 4):
        lhs = jnp.concatenate(
            [slb[pl.ds(p + i, 3)].reshape(9 * CS, VOX) for i in range(4)], axis=1
        )
        rhs = jnp.concatenate([xc[p + i] for i in range(4)], axis=1)
        part = lax.dot_general(lhs, rhs, (((1,), (1,)), ((), ())), preferred_element_type=F32)
        acc[...] = part if p == 0 else acc[...] + part

    for a in range(3):
        for b in range(3):
            rows = acc[pl.ds(((2 - a) * 3 + b) * CS, CS), :]
            for cc in range(3):
                part = rows[:, cc * 64 : cc * 64 + 64]
                kg_ref[a * 9 + b * 3 + cc] = part

    k_out.wait_send()
    for own, sem in ((self_a, a_send), (self_a, r_send)):
        @pl.when(own)
        def _():
            taken(xh.at[pl.ds(0, 15 * CS)], sem)

        @pl.when(jnp.logical_not(own))
        def _():
            taken(xh, sem)

    @pl.when(self_v)
    def _():
        taken(v2.at[pl.ds(0, 7)], v_send)

    @pl.when(jnp.logical_not(self_v))
    def _():
        taken(v2.at[pl.ds(0, 8)], v_send)

    taken(v2.at[pl.ds(0, 8)], f_send)
    taken(psend.at[1, 1], p_send.at[2])

    @pl.when(not_last)
    def _():
        for r in range(2):
            taken(psend.at[0, r], p_send.at[3 + r])
        taken(mine, n_send.at[2])

    @pl.when(not_first)
    def _():
        for r in range(2):
            taken(psend.at[2, r], p_send.at[5 + r])
        taken(mine, n_send.at[0])

    taken(mine, n_send.at[1])

    own_copies(sent)
    own_along(sent)
    passed_on(sent, lambda p: None)

    taken(rs, r_recv)
    total = rs[0].astype(F32)
    for j in range(1, 16):
        total = total + rs[j].astype(F32)
    ig_ref[...] = total.T.astype(BF16)


def local(volume, cotangent, kernel):
    in_hbm = pl.BlockSpec(memory_space=pltpu.HBM)
    in_vmem = pl.BlockSpec(memory_space=pltpu.VMEM)
    dma = pltpu.SemaphoreType.DMA
    ig, kg = pl.pallas_call(
        kernel_body,
        out_shape=(
            jax.ShapeDtypeStruct((VOX, CS), BF16),
            jax.ShapeDtypeStruct((TAPS, CS, 64), F32),
        ),
        in_specs=[in_hbm] * 3,
        out_specs=(in_vmem, in_vmem),
        scratch_shapes=[
            pltpu.VMEM((VOX, CS), BF16),
            pltpu.VMEM((VOX, CS), BF16),
            pltpu.VMEM((CS, VOX), BF16),
            pltpu.VMEM((HALF, VOX), BF16),
                    pltpu.VMEM((28, O2, HALF), BF16),
            pltpu.VMEM((HALF, TPAD), BF16),
            pltpu.VMEM((3, 2, CS, VOX), BF16),
            pltpu.VMEM((3, 2, CS, VOX), BF16),
            pltpu.VMEM((CS, VOX), F32),
            pltpu.VMEM((ND + 2, CS, VOX), BF16),
            pltpu.VMEM((3, CS, VOX), BF16),
            pltpu.VMEM((TPAD, VOX), BF16),
            pltpu.VMEM((HALF, VOX), BF16),
            pltpu.VMEM((16, CS, VOX), BF16),
            pltpu.VMEM((ND, 64, VOX), BF16),
            pltpu.VMEM((ND, 192, VOX), BF16),
            pltpu.VMEM((ND + 2, 3 * CS, VOX), BF16),
            pltpu.VMEM((9 * CS, 192), F32),
            dma((3,)), dma, dma, dma, dma((2,)), dma((7,)), dma((3, 2)), dma((32,)), dma((ND,)),
            dma((3,)), dma((3,)), dma, dma((ND,)), dma, dma, dma,
        ],
        compiler_params=pltpu.CompilerParams(
            collective_id=0, has_side_effects=True, vmem_limit_bytes=48 * 2**20
        ),
        cost_estimate=pl.CostEstimate(
            flops=3 * 453_000_000, bytes_accessed=6_000_000, transcendentals=8192
        ),
    )(
        pltpu.with_memory_space_constraint(volume.reshape(VOX, CS), pltpu.HBM),
        pltpu.with_memory_space_constraint(cotangent.reshape(VOX, CS), pltpu.HBM),
        pltpu.with_memory_space_constraint(jnp.transpose(kernel, (1, 0, 2)), pltpu.HBM),
    )
    ig, kg = pl.pallas_call(
        finish,
        out_shape=(
            jax.ShapeDtypeStruct((VOX, CS), BF16),
            jax.ShapeDtypeStruct((TAPS, CS, 64), F32),
        ),
        in_specs=[pl.BlockSpec(memory_space=pl.ANY)] * 2,
        out_specs=(pl.BlockSpec(memory_space=pl.ANY),) * 2,
        scratch_shapes=[dma((2,))],
    )(*(pltpu.with_memory_space_constraint(v, pltpu.VMEM) for v in (ig, kg)))
    input_grad = ig.reshape(1, SIDE, SIDE, CS)
    kernel_grad = jnp.transpose(kg, (1, 0, 2))[None]
    return (input_grad, kernel_grad)


def solution(mesh):
    return jax.shard_map(
        local,
        mesh=mesh,
        in_specs=(
            P("depth", None, None, "chan"),
            P("depth", None, None, "chan"),
            P("chan", None, None),
        ),
        out_specs=(P("depth", None, None, "chan"), P("chan", None, None, "depth")),
        check_vma=False,
    )
```

```python
import functools

import jax
import jax.numpy as jnp
from jax import lax
from jax.experimental import pallas as pl
from jax.experimental.pallas import tpu as pltpu
from jax.sharding import PartitionSpec as P

MESH = pl.DeviceIdType.MESH
F32, BF16 = jnp.float32, jnp.bfloat16
ND, NX, NL, NZ, NK = 16, 4, 4, 8, 32
CS, SIDE, VOX, CH = 32, 16, 256, 1024
HALF, TAPS, O2 = 512, 27, 64
TROWS, TPAD = TAPS * O2, 28 * O2


def finish(ig_ref, kg_ref, ig_out, kg_out, sem):
    a = pltpu.make_async_copy(ig_ref, ig_out, sem.at[0])
    b = pltpu.make_async_copy(kg_ref, kg_out, sem.at[1])
    b.start()
    a.start()
    a.wait()
    b.wait()


def kernel_body(
    vol_hbm, cot_hbm, k_hbm, ig_ref, kg_ref,
    vin, cin, xt, xh, k2, kt, psend, prec, held, sl, ss, cm, og, rs, v2, xc, slb, acc,
    in_sem, k_send, k_recv, a_send, a_recv, p_send, p_recv, s_send, s_recv, n_send, n_recv,
    v_send, v_recv, f_send, r_send, r_recv,
):
    d, k = lax.axis_index("depth"), lax.axis_index("chan")
    x, zl = d // NL, d % NL
    y, zh, c, m = k // 4, (k // 2) % 2, k % 2, k // 2
    z, sib = zh * NL + zl, k + 1 - 2 * c
    khalf = k // 16
    self_a = khalf == c
    self_v = jnp.logical_and(zl % 2 == c, x // 2 == c)

    def remote(src, dst, ssem, rsem, dev):
        return pltpu.make_async_remote_copy(
            src_ref=src, dst_ref=dst, send_sem=ssem, recv_sem=rsem, device_id=dev,
            device_id_type=MESH,
        )

    def taken(ref, sem):
        pltpu.make_async_copy(ref, ref, sem).wait()

    vol_in = pltpu.make_async_copy(vol_hbm, vin, in_sem.at[0])
    cot_in = pltpu.make_async_copy(cot_hbm, cin, in_sem.at[1])
    k_in = pltpu.make_async_copy(
        k_hbm.at[:, :, pl.ds(pl.multiple_of(c * HALF, HALF), HALF)],
        k2.at[pl.ds(0, TAPS), pl.ds(0, CS)], in_sem.at[2],
    )
    vol_in.start()
    cot_in.start()
    k_in.start()

    bar = pltpu.get_barrier_semaphore()

    def greet(dd, kk):
        pl.semaphore_signal(bar, inc=1, device_id=(dd, kk), device_id_type=MESH)

    def far_first(j):
        i = j % 8
        dy = 4 + jnp.where(i % 2 == 1, -((i + 1) // 2), i // 2)
        yy = (y + dy) % 8
        return yy, yy * 2 + jnp.where(j < 8, 1 - zh, zh)

    @pl.loop(0, 16)
    def _(j):
        yy, mm = far_first(j)
        mine = 2 * mm + khalf

        @pl.when(mine != k)
        def _():
            greet(d, mine)

        @pl.when(jnp.logical_and(yy // 4 == c, mine + 1 - 2 * khalf != k))
        def _():
            greet(d, mine + 1 - 2 * khalf)

    @pl.loop(1, 4)
    def _(j):
        greet((x + j) % NX * NL + zl, k)
        greet(x * NL + (zl + j) % NL, k)

    for kk in (k, sib):
        greet((d + 1) % ND, kk)
        greet((d + ND - 1) % ND, kk)

    odd = (z + c) % 2

    @pl.loop(0, 8)
    def _(j):
        xs, t = j // 2, j % 2
        step = jnp.where(odd == 1, 2 * t - 1, t * (2 - 4 * (xs % 2)))
        zs = (z - step + NZ) % NZ
        dd, kk = xs * NL + zs % NL, (y * 2 + zs // NL) * 2 + x // 2

        @pl.when(jnp.logical_or(dd != d, kk != k))
        def _():
            greet(dd, kk)

    vol_in.wait()
    xt[...] = vin[...].astype(F32).T.astype(BF16)

    zero = jnp.zeros((CS, VOX), BF16)
    slb[0] = jnp.zeros((3 * CS, VOX), BF16)
    slb[ND + 1] = jnp.zeros((3 * CS, VOX), BF16)
    sl[0] = zero
    sl[ND + 1] = zero
    cm[pl.ds(TROWS, O2), :] = jnp.zeros((O2, VOX), BF16)
    k2[TAPS] = jnp.zeros((O2, HALF), BF16)

    @pl.when(d == 0)
    def _():
        prec[0] = jnp.zeros((2, CS, VOX), BF16)
        ss[0] = zero

    @pl.when(d == ND - 1)
    def _():
        prec[2] = jnp.zeros((2, CS, VOX), BF16)
        ss[2] = zero

    sa, sv = self_a.astype(jnp.int32), self_v.astype(jnp.int32)
    pl.semaphore_wait(bar, 24 - sa + 6 + 4 + 8 - sv)

    a_slot = xh.at[pl.ds(pl.multiple_of((k % 16) * CS, CS), CS)]

    @pl.loop(0, 16)
    def _(j):
        to = 2 * far_first(j)[1] + khalf

        @pl.when(to != k)
        def _():
            remote(xt, a_slot, a_send, a_recv.at[zh], (d, to)).start()

        @pl.when(to == k)
        def _():
            pltpu.make_async_copy(xt, a_slot, a_recv.at[zh]).start()

    k_out = remote(
        k_hbm.at[:, :, pl.ds(pl.multiple_of((1 - c) * HALF, HALF), HALF)],
        k2.at[pl.ds(0, TAPS), pl.ds(CS, CS)], k_send, k_recv, (d, sib),
    )
    k_out.start()

    k_in.wait()
    k_out.wait_recv()
    for p in range(14):
        kt[:, pl.ds(p * 128, 128)] = k2[pl.ds(2 * p, 2)].reshape(128, HALF).T

    lane = lax.broadcasted_iota(jnp.int32, (1, VOX), 1)
    hh, ww = lane // SIDE, lane % SIDE
    h_lo, h_hi = hh >= 1, hh <= SIDE - 2
    w_lo, w_hi = ww >= 1, ww <= SIDE - 2

    def moved(v, step, keep):
        return jnp.where(keep, pltpu.roll(v, step % VOX, 1), 0.0)

    def up(v):
        return moved(v, SIDE, h_lo)

    def down(v):
        return moved(v, -SIDE, h_hi)

    def right(v):
        return moved(v, 1, w_lo)

    def left(v):
        return moved(v, -1, w_hi)

    def spread_out(other):
      @pl.loop(0, 4)
      def _(j):
        xd, t = 2 * c + j % 2, j // 2
        even = (z + zh + other) % 2 == 0
        step = jnp.where(even, (1 - t) * (2 - 4 * (x % 2)), 2 * t - 1)
        zd = (z + step + NZ) % NZ
        dd, kk = xd * NL + zd % NL, (y * 2 + zd // NL) * 2 + zl % 2
        src = xh.at[pl.ds(pl.multiple_of(((j % 2) * NL + zd % NL) * 64, 64), 64)]
        own = jnp.logical_and(dd == d, kk == k)

        @pl.when(jnp.logical_not(own))
        def _():
            remote(src, v2.at[d], v_send, v_recv.at[d], (dd, kk)).start()

        @pl.when(own)
        def _():
            pltpu.make_async_copy(src, v2.at[d], v_recv.at[d]).start()

    taken(xh.at[pl.ds(0, 8 * CS)], a_recv.at[zh])
    spread_out(0)
    taken(xh.at[pl.ds(0, 8 * CS)], a_recv.at[1 - zh])
    xv = xh[...]

    for a in (0, 2, 1):
        yv = jnp.dot(k2[pl.ds(a * 9, 9)].reshape(9 * O2, HALF), xv, preferred_element_type=F32)

        def tap(b, cc):
            at = (b * 3 + cc) * O2
            return yv[at : at + O2, :]

        cols = [tap(1, cc) + up(tap(0, cc)) + down(tap(2, cc)) for cc in range(3)]
        tot = cols[1] + right(cols[0]) + left(cols[2])
        if a == 1:
            held[...] = tot[:CS]
            psend[a, 1] = tot[CS:].astype(BF16)
            remote(psend.at[1, 1], prec.at[1, c], p_send.at[2], p_recv.at[1, c], (d, sib)).start()
        else:
            psend[a, 0] = tot[:CS].astype(BF16)
            psend[a, 1] = tot[CS:].astype(BF16)
            i = 0 if a == 0 else 1
            there = d + 1 - a

            @pl.when(jnp.logical_and(there >= 0, there < ND))
            def _():
                for r, kk in ((0, k), (1, sib)):
                    remote(
                        psend.at[a, r], prec.at[a, c], p_send.at[3 + 2 * i + r], p_recv.at[a, c],
                        (there, kk),
                    ).start()

    spread_out(1)

    cot_in.wait()
    cot_t = cin[...].astype(F32).T
    not_first, not_last = d >= 1, d <= ND - 2
    taken(prec.at[1, 1 - c], p_recv.at[1, 1 - c])

    @pl.when(not_first)
    def _():
        taken(prec.at[0, 0], p_recv.at[0, 0])
        taken(prec.at[0, 1], p_recv.at[0, 1])

    @pl.when(not_last)
    def _():
        taken(prec.at[2, 0], p_recv.at[2, 0])
        taken(prec.at[2, 1], p_recv.at[2, 1])

    got = [prec[1, 1 - c], prec[0, 0], prec[0, 1], prec[2, 0], prec[2, 1]]
    pre = held[...] + sum(v.astype(F32) for v in got)
    sig = 1.0 / (1.0 + jnp.exp(-pre))
    sl[d + 1] = (cot_t * sig * (1.0 + pre * (1.0 - sig))).astype(BF16)

    mine = sl.at[d + 1]

    def slope_out(plane, to, i):
        at = sl.at[plane + 1]
        return remote(at, at, s_send.at[i], s_recv.at[plane], (to, k))

    far_up, far_down = jnp.logical_and(zl == 3, not_last), jnp.logical_and(zl == 0, not_first)

    def own_copies(act):
        @pl.when(far_up)
        def _():
            act(d, d + 1, 8)

        @pl.when(far_down)
        def _():
            act(d, d - 1, 9)

        @pl.when(zl < NL - 1)
        def _():
            act(d, d + 1, zl + 1)

        @pl.when(zl > 0)
        def _():
            act(d, d - 1, zl - 1)

    def own_along(act):
        @pl.loop(0, NL)
        def _(t):
            @pl.when(jnp.logical_or(t < zl - 1, t > zl + 1))
            def _():
                act(d, x * NL + t, t)

        @pl.loop(0, NX)
        def _(t):
            @pl.when(t != x)
            def _():
                act(d, t * NL + zl, 4 + t)

    def passed_on(act, first):
        @pl.loop(0, NL)
        def _(zs):
            p = x * NL + zs

            @pl.when(zs != zl)
            def _():
                first(p)

                @pl.loop(0, NX)
                def _(t):
                    to = t * NL + zl
                    near = jnp.logical_or(to == p + 1, to == p - 1)

                    @pl.when(jnp.logical_and(t != x, jnp.logical_not(near)))
                    def _():
                        act(p, to, 16 + zs * NX + t)

    def send(plane, to, i):
        slope_out(plane, to, i).start()

    def sent(plane, to, i):
        taken(mine, s_send.at[i])

    own_copies(send)
    remote(mine, ss.at[1], n_send.at[1], n_recv.at[1], (d, sib)).start()

    @pl.when(not_first)
    def _():
        remote(mine, ss.at[2], n_send.at[0], n_recv.at[2], (d - 1, sib)).start()

    @pl.when(not_last)
    def _():
        remote(mine, ss.at[0], n_send.at[2], n_recv.at[0], (d + 1, sib)).start()

    def columns(a):
        s = jnp.concatenate([sl[d + 2 - a], ss[2 - a]], axis=0).astype(F32)
        for cc, sc in ((1, s), (0, left(s)), (2, right(s))):
            for b, sb in ((1, sc), (0, down(sc)), (2, up(sc))):
                cm[pl.ds((a * 9 + b * 3 + cc) * O2, O2), :] = sb.astype(BF16)

    taken(ss.at[1], n_recv.at[1])
    columns(1)
    own_along(send)

    @pl.when(not_first)
    def _():
        taken(sl.at[d], s_recv.at[d - 1])
        taken(ss.at[0], n_recv.at[0])

    @pl.when(not_last)
    def _():
        taken(sl.at[d + 2], s_recv.at[d + 1])
        taken(ss.at[2], n_recv.at[2])

    columns(0)
    columns(2)

    r_slot = rs.at[m]

    @pl.loop(0, 2)
    def _(n):
        zd = jnp.where(n == 0, 1 - zh, zh)
        lhs = jnp.concatenate(
            [kt[pl.ds(pl.multiple_of(i * 128 + zd * 64, 64), 64), :] for i in range(4)], axis=0
        )
        part = jnp.dot(lhs, cm[...], preferred_element_type=F32).astype(BF16)
        for i in range(4):
            og[pl.ds(pl.multiple_of(i * 128 + zd * 64, 64), 64), :] = part[i * 64 : i * 64 + 64]

        @pl.loop(0, 8)
        def _(i):
            far = (y + i // 2 + jnp.where(khalf == c, 2, 0)) % 4
            j = far * 4 + zd * 2 + i % 2
            to = 16 * c + j
            src = og.at[pl.ds(pl.multiple_of(j * CS, CS), CS)]

            @pl.when(to != k)
            def _():
                remote(src, r_slot, r_send, r_recv, (d, to)).start()

            @pl.when(to == k)
            def _():
                pltpu.make_async_copy(src, r_slot, r_recv).start()

    def arrived(p):
        @pl.when(jnp.logical_or(p < d - 1, p > d + 1))
        def _():
            taken(sl.at[p + 1], s_recv.at[p])

    passed_on(send, arrived)

    def spread_chans(odd_plane, forward):
        @pl.loop(0, 8, unroll=2)
        def _(j):
            p = (j // 2) * NL + 2 * (j % 2) + odd_plane
            taken(v2.at[p], v_recv.at[p])
            if forward:
                remote(v2.at[p], v2.at[p], f_send, v_recv.at[p], (d, sib)).start()
            v = v2[p].astype(F32)
            xc[p, pl.ds(0, 64), :] = right(v).astype(BF16)
            xc[p, pl.ds(64, 64), :] = v2[p]
            xc[p, pl.ds(128, 64), :] = left(v).astype(BF16)

    spread_chans(c, True)

    spread_chans(1 - c, False)

    @pl.loop(0, ND)
    def _(p):
        @pl.when(p // NL != x)
        def _():
            arrived(p)

    @pl.loop(0, ND, unroll=4)
    def _(p):
        v = sl[p + 1].astype(F32)
        slb[p + 1, pl.ds(0, CS), :] = down(v).astype(BF16)
        slb[p + 1, pl.ds(CS, CS), :] = sl[p + 1]
        slb[p + 1, pl.ds(2 * CS, CS), :] = up(v).astype(BF16)

    for p in range(0, ND, 4):
        lhs = jnp.concatenate(
            [slb[pl.ds(p + i, 3)].reshape(9 * CS, VOX) for i in range(4)], axis=1
        )
        rhs = jnp.concatenate([xc[p + i] for i in range(4)], axis=1)
        part = lax.dot_general(lhs, rhs, (((1,), (1,)), ((), ())), preferred_element_type=F32)
        acc[...] = part if p == 0 else acc[...] + part

    for a in range(3):
        for b in range(3):
            rows = acc[pl.ds(((2 - a) * 3 + b) * CS, CS), :]
            for cc in range(3):
                part = rows[:, cc * 64 : cc * 64 + 64]
                kg_ref[a * 9 + b * 3 + cc] = part

    k_out.wait_send()
    for own, sem in ((self_a, a_send), (self_a, r_send)):
        @pl.when(own)
        def _():
            taken(xh.at[pl.ds(0, 15 * CS)], sem)

        @pl.when(jnp.logical_not(own))
        def _():
            taken(xh, sem)

    @pl.when(self_v)
    def _():
        taken(v2.at[pl.ds(0, 7)], v_send)

    @pl.when(jnp.logical_not(self_v))
    def _():
        taken(v2.at[pl.ds(0, 8)], v_send)

    taken(v2.at[pl.ds(0, 8)], f_send)
    taken(psend.at[1, 1], p_send.at[2])

    @pl.when(not_last)
    def _():
        for r in range(2):
            taken(psend.at[0, r], p_send.at[3 + r])
        taken(mine, n_send.at[2])

    @pl.when(not_first)
    def _():
        for r in range(2):
            taken(psend.at[2, r], p_send.at[5 + r])
        taken(mine, n_send.at[0])

    taken(mine, n_send.at[1])

    own_copies(sent)
    own_along(sent)
    passed_on(sent, lambda p: None)

    taken(rs, r_recv)
    total = rs[0].astype(F32)
    for j in range(1, 16):
        total = total + rs[j].astype(F32)
    ig_ref[...] = total.T.astype(BF16)


def local(volume, cotangent, kernel):
    in_hbm = pl.BlockSpec(memory_space=pltpu.HBM)
    in_vmem = pl.BlockSpec(memory_space=pltpu.VMEM)
    dma = pltpu.SemaphoreType.DMA
    ig, kg = pl.pallas_call(
        kernel_body,
        out_shape=(
            jax.ShapeDtypeStruct((VOX, CS), BF16),
            jax.ShapeDtypeStruct((TAPS, CS, 64), F32),
        ),
        in_specs=[in_hbm] * 3,
        out_specs=(in_vmem, in_vmem),
        scratch_shapes=[
            pltpu.VMEM((VOX, CS), BF16),
            pltpu.VMEM((VOX, CS), BF16),
            pltpu.VMEM((CS, VOX), BF16),
            pltpu.VMEM((HALF, VOX), BF16),
                    pltpu.VMEM((28, O2, HALF), BF16),
            pltpu.VMEM((HALF, TPAD), BF16),
            pltpu.VMEM((3, 2, CS, VOX), BF16),
            pltpu.VMEM((3, 2, CS, VOX), BF16),
            pltpu.VMEM((CS, VOX), F32),
            pltpu.VMEM((ND + 2, CS, VOX), BF16),
            pltpu.VMEM((3, CS, VOX), BF16),
            pltpu.VMEM((TPAD, VOX), BF16),
            pltpu.VMEM((HALF, VOX), BF16),
            pltpu.VMEM((16, CS, VOX), BF16),
            pltpu.VMEM((ND, 64, VOX), BF16),
            pltpu.VMEM((ND, 192, VOX), BF16),
            pltpu.VMEM((ND + 2, 3 * CS, VOX), BF16),
            pltpu.VMEM((9 * CS, 192), F32),
            dma((3,)), dma, dma, dma, dma((2,)), dma((7,)), dma((3, 2)), dma((32,)), dma((ND,)),
            dma((3,)), dma((3,)), dma, dma((ND,)), dma, dma, dma,
        ],
        compiler_params=pltpu.CompilerParams(
            collective_id=0, has_side_effects=True, vmem_limit_bytes=48 * 2**20
        ),
        cost_estimate=pl.CostEstimate(
            flops=3 * 453_000_000, bytes_accessed=6_000_000, transcendentals=8192
        ),
    )(
        pltpu.with_memory_space_constraint(volume.reshape(VOX, CS), pltpu.HBM),
        pltpu.with_memory_space_constraint(cotangent.reshape(VOX, CS), pltpu.HBM),
        pltpu.with_memory_space_constraint(jnp.transpose(kernel, (1, 0, 2)), pltpu.HBM),
    )
    ig, kg = pl.pallas_call(
        finish,
        out_shape=(
            jax.ShapeDtypeStruct((VOX, CS), BF16),
            jax.ShapeDtypeStruct((TAPS, CS, 64), F32),
        ),
        in_specs=[pl.BlockSpec(memory_space=pl.ANY)] * 2,
        out_specs=(pl.BlockSpec(memory_space=pl.ANY),) * 2,
        scratch_shapes=[dma((2,))],
    )(*(pltpu.with_memory_space_constraint(v, pltpu.VMEM) for v in (ig, kg)))
    input_grad = ig.reshape(1, SIDE, SIDE, CS)
    kernel_grad = jnp.transpose(kg, (1, 0, 2))[None]
    return (input_grad, kernel_grad)


def solution(mesh):
    return jax.shard_map(
        local,
        mesh=mesh,
        in_specs=(
            P("depth", None, None, "chan"),
            P("depth", None, None, "chan"),
            P("chan", None, None),
        ),
        out_specs=(P("depth", None, None, "chan"), P("chan", None, None, "depth")),
        check_vma=False,
    )
```

```python
import functools

import jax
import jax.numpy as jnp
from jax import lax
from jax.experimental import pallas as pl
from jax.experimental.pallas import tpu as pltpu
from jax.sharding import PartitionSpec as P

MESH = pl.DeviceIdType.MESH
F32, BF16 = jnp.float32, jnp.bfloat16
ND, NX, NL, NZ, NK = 16, 4, 4, 8, 32
CS, SIDE, VOX, CH = 32, 16, 256, 1024
HALF, TAPS, O2 = 512, 27, 64
TROWS, TPAD = TAPS * O2, 28 * O2


def finish(ig_ref, kg_ref, ig_out, kg_out, sem):
    a = pltpu.make_async_copy(ig_ref, ig_out, sem.at[0])
    b = pltpu.make_async_copy(kg_ref, kg_out, sem.at[1])
    b.start()
    a.start()
    a.wait()
    b.wait()


def kernel_body(
    vol_hbm, cot_hbm, k_hbm, ig_ref, kg_ref,
    vin, cin, xt, xh, k2, kt, psend, prec, held, sl, ss, cm, og, rs, v2, xc, slb, acc,
    in_sem, k_send, k_recv, a_send, a_recv, p_send, p_recv, s_send, s_recv, n_send, n_recv,
    v_send, v_recv, f_send, r_send, r_recv,
):
    d, k = lax.axis_index("depth"), lax.axis_index("chan")
    x, zl = d // NL, d % NL
    y, zh, c, m = k // 4, (k // 2) % 2, k % 2, k // 2
    z, sib = zh * NL + zl, k + 1 - 2 * c
    khalf = k // 16
    self_a = khalf == c
    self_v = jnp.logical_and(zl % 2 == c, x // 2 == c)

    def remote(src, dst, ssem, rsem, dev):
        return pltpu.make_async_remote_copy(
            src_ref=src, dst_ref=dst, send_sem=ssem, recv_sem=rsem, device_id=dev,
            device_id_type=MESH,
        )

    def taken(ref, sem):
        pltpu.make_async_copy(ref, ref, sem).wait()

    vol_in = pltpu.make_async_copy(vol_hbm, vin, in_sem.at[0])
    cot_in = pltpu.make_async_copy(cot_hbm, cin, in_sem.at[1])
    k_in = pltpu.make_async_copy(
        k_hbm.at[:, :, pl.ds(pl.multiple_of(c * HALF, HALF), HALF)],
        k2.at[pl.ds(0, TAPS), pl.ds(0, CS)], in_sem.at[2],
    )
    vol_in.start()
    cot_in.start()
    k_in.start()

    bar = pltpu.get_barrier_semaphore()

    def greet(dd, kk):
        pl.semaphore_signal(bar, inc=1, device_id=(dd, kk), device_id_type=MESH)

    def far_first(j):
        i = j % 8
        dy = 4 + jnp.where(i % 2 == 1, -((i + 1) // 2), i // 2)
        yy = (y + dy) % 8
        return yy, yy * 2 + jnp.where(j < 8, 1 - zh, zh)

    @pl.loop(0, 16)
    def _(j):
        yy, mm = far_first(j)
        mine = 2 * mm + khalf

        @pl.when(mine != k)
        def _():
            greet(d, mine)

        @pl.when(jnp.logical_and(yy // 4 == c, mine + 1 - 2 * khalf != k))
        def _():
            greet(d, mine + 1 - 2 * khalf)

    @pl.loop(1, 4)
    def _(j):
        greet((x + j) % NX * NL + zl, k)
        greet(x * NL + (zl + j) % NL, k)

    for kk in (k, sib):
        greet((d + 1) % ND, kk)
        greet((d + ND - 1) % ND, kk)

    odd = (z + c) % 2

    @pl.loop(0, 8)
    def _(j):
        xs, t = j // 2, j % 2
        step = jnp.where(odd == 1, 2 * t - 1, t * (2 - 4 * (xs % 2)))
        zs = (z - step + NZ) % NZ
        dd, kk = xs * NL + zs % NL, (y * 2 + zs // NL) * 2 + x // 2

        @pl.when(jnp.logical_or(dd != d, kk != k))
        def _():
            greet(dd, kk)

    vol_in.wait()
    xt[...] = vin[...].astype(F32).T.astype(BF16)

    zero = jnp.zeros((CS, VOX), BF16)
    slb[0] = jnp.zeros((3 * CS, VOX), BF16)
    slb[ND + 1] = jnp.zeros((3 * CS, VOX), BF16)
    sl[0] = zero
    sl[ND + 1] = zero
    cm[pl.ds(TROWS, O2), :] = jnp.zeros((O2, VOX), BF16)
    k2[TAPS] = jnp.zeros((O2, HALF), BF16)

    @pl.when(d == 0)
    def _():
        prec[0] = jnp.zeros((2, CS, VOX), BF16)
        ss[0] = zero

    @pl.when(d == ND - 1)
    def _():
        prec[2] = jnp.zeros((2, CS, VOX), BF16)
        ss[2] = zero

    sa, sv = self_a.astype(jnp.int32), self_v.astype(jnp.int32)
    pl.semaphore_wait(bar, 24 - sa + 6 + 4 + 8 - sv)

    a_slot = xh.at[pl.ds(pl.multiple_of((k % 16) * CS, CS), CS)]

    @pl.loop(0, 16)
    def _(j):
        to = 2 * far_first(j)[1] + khalf

        @pl.when(to != k)
        def _():
            remote(xt, a_slot, a_send, a_recv.at[zh], (d, to)).start()

        @pl.when(to == k)
        def _():
            pltpu.make_async_copy(xt, a_slot, a_recv.at[zh]).start()

    k_out = remote(
        k_hbm.at[:, :, pl.ds(pl.multiple_of((1 - c) * HALF, HALF), HALF)],
        k2.at[pl.ds(0, TAPS), pl.ds(CS, CS)], k_send, k_recv, (d, sib),
    )
    k_out.start()

    k_in.wait()
    k_out.wait_recv()
    for p in range(14):
        kt[:, pl.ds(p * 128, 128)] = k2[pl.ds(2 * p, 2)].reshape(128, HALF).T

    lane = lax.broadcasted_iota(jnp.int32, (1, VOX), 1)
    hh, ww = lane // SIDE, lane % SIDE
    h_lo, h_hi = hh >= 1, hh <= SIDE - 2
    w_lo, w_hi = ww >= 1, ww <= SIDE - 2

    def moved(v, step, keep):
        return jnp.where(keep, pltpu.roll(v, step % VOX, 1), 0.0)

    def up(v):
        return moved(v, SIDE, h_lo)

    def down(v):
        return moved(v, -SIDE, h_hi)

    def right(v):
        return moved(v, 1, w_lo)

    def left(v):
        return moved(v, -1, w_hi)

    def spread_out(other):
      @pl.loop(0, 4)
      def _(j):
        xd, t = 2 * c + j % 2, j // 2
        even = (z + zh + other) % 2 == 0
        step = jnp.where(even, (1 - t) * (2 - 4 * (x % 2)), 2 * t - 1)
        zd = (z + step + NZ) % NZ
        dd, kk = xd * NL + zd % NL, (y * 2 + zd // NL) * 2 + zl % 2
        src = xh.at[pl.ds(pl.multiple_of(((j % 2) * NL + zd % NL) * 64, 64), 64)]
        own = jnp.logical_and(dd == d, kk == k)

        @pl.when(jnp.logical_not(own))
        def _():
            remote(src, v2.at[d], v_send, v_recv.at[d], (dd, kk)).start()

        @pl.when(own)
        def _():
            pltpu.make_async_copy(src, v2.at[d], v_recv.at[d]).start()

    taken(xh.at[pl.ds(0, 8 * CS)], a_recv.at[zh])
    spread_out(0)
    taken(xh.at[pl.ds(0, 8 * CS)], a_recv.at[1 - zh])
    xv = xh[...]

    for a in (0, 2, 1):
        yv = jnp.dot(k2[pl.ds(a * 9, 9)].reshape(9 * O2, HALF), xv, preferred_element_type=F32)

        def tap(b, cc):
            at = (b * 3 + cc) * O2
            return yv[at : at + O2, :]

        cols = [tap(1, cc) + up(tap(0, cc)) + down(tap(2, cc)) for cc in range(3)]
        tot = cols[1] + right(cols[0]) + left(cols[2])
        if a == 1:
            held[...] = tot[:CS]
            psend[a, 1] = tot[CS:].astype(BF16)
            remote(psend.at[1, 1], prec.at[1, c], p_send.at[2], p_recv.at[1, c], (d, sib)).start()
        else:
            psend[a, 0] = tot[:CS].astype(BF16)
            psend[a, 1] = tot[CS:].astype(BF16)
            i = 0 if a == 0 else 1
            there = d + 1 - a

            @pl.when(jnp.logical_and(there >= 0, there < ND))
            def _():
                for r, kk in ((0, k), (1, sib)):
                    remote(
                        psend.at[a, r], prec.at[a, c], p_send.at[3 + 2 * i + r], p_recv.at[a, c],
                        (there, kk),
                    ).start()

    spread_out(1)

    cot_in.wait()
    cot_t = cin[...].astype(F32).T
    not_first, not_last = d >= 1, d <= ND - 2
    taken(prec.at[1, 1 - c], p_recv.at[1, 1 - c])

    @pl.when(not_first)
    def _():
        taken(prec.at[0, 0], p_recv.at[0, 0])
        taken(prec.at[0, 1], p_recv.at[0, 1])

    @pl.when(not_last)
    def _():
        taken(prec.at[2, 0], p_recv.at[2, 0])
        taken(prec.at[2, 1], p_recv.at[2, 1])

    got = [prec[1, 1 - c], prec[0, 0], prec[0, 1], prec[2, 0], prec[2, 1]]
    pre = held[...] + sum(v.astype(F32) for v in got)
    sig = 1.0 / (1.0 + jnp.exp(-pre))
    sl[d + 1] = (cot_t * sig * (1.0 + pre * (1.0 - sig))).astype(BF16)

    mine = sl.at[d + 1]

    def slope_out(plane, to, i):
        at = sl.at[plane + 1]
        return remote(at, at, s_send.at[i], s_recv.at[plane], (to, k))

    far_up, far_down = jnp.logical_and(zl == 3, not_last), jnp.logical_and(zl == 0, not_first)

    def own_copies(act):
        @pl.when(far_up)
        def _():
            act(d, d + 1, 8)

        @pl.when(far_down)
        def _():
            act(d, d - 1, 9)

        @pl.when(zl < NL - 1)
        def _():
            act(d, d + 1, zl + 1)

        @pl.when(zl > 0)
        def _():
            act(d, d - 1, zl - 1)

    def own_along(act):
        @pl.loop(0, NL)
        def _(t):
            @pl.when(jnp.logical_or(t < zl - 1, t > zl + 1))
            def _():
                act(d, x * NL + t, t)

        @pl.loop(0, NX)
        def _(t):
            @pl.when(t != x)
            def _():
                act(d, t * NL + zl, 4 + t)

    def passed_on(act, first):
        @pl.loop(0, NL)
        def _(zs):
            p = x * NL + zs

            @pl.when(zs != zl)
            def _():
                first(p)

                @pl.loop(0, NX)
                def _(t):
                    to = t * NL + zl
                    near = jnp.logical_or(to == p + 1, to == p - 1)

                    @pl.when(jnp.logical_and(t != x, jnp.logical_not(near)))
                    def _():
                        act(p, to, 16 + zs * NX + t)

    def send(plane, to, i):
        slope_out(plane, to, i).start()

    def sent(plane, to, i):
        taken(mine, s_send.at[i])

    own_copies(send)
    remote(mine, ss.at[1], n_send.at[1], n_recv.at[1], (d, sib)).start()

    @pl.when(not_first)
    def _():
        remote(mine, ss.at[2], n_send.at[0], n_recv.at[2], (d - 1, sib)).start()

    @pl.when(not_last)
    def _():
        remote(mine, ss.at[0], n_send.at[2], n_recv.at[0], (d + 1, sib)).start()

    def columns(a):
        s = jnp.concatenate([sl[d + 2 - a], ss[2 - a]], axis=0).astype(F32)
        for cc, sc in ((1, s), (0, left(s)), (2, right(s))):
            for b, sb in ((1, sc), (0, down(sc)), (2, up(sc))):
                cm[pl.ds((a * 9 + b * 3 + cc) * O2, O2), :] = sb.astype(BF16)

    taken(ss.at[1], n_recv.at[1])
    columns(1)

    @pl.when(not_first)
    def _():
        taken(sl.at[d], s_recv.at[d - 1])
        taken(ss.at[0], n_recv.at[0])

    @pl.when(not_last)
    def _():
        taken(sl.at[d + 2], s_recv.at[d + 1])
        taken(ss.at[2], n_recv.at[2])

    own_along(send)
    columns(0)
    columns(2)

    r_slot = rs.at[m]

    @pl.loop(0, 2)
    def _(n):
        zd = jnp.where(n == 0, 1 - zh, zh)
        lhs = jnp.concatenate(
            [kt[pl.ds(pl.multiple_of(i * 128 + zd * 64, 64), 64), :] for i in range(4)], axis=0
        )
        part = jnp.dot(lhs, cm[...], preferred_element_type=F32).astype(BF16)
        for i in range(4):
            og[pl.ds(pl.multiple_of(i * 128 + zd * 64, 64), 64), :] = part[i * 64 : i * 64 + 64]

        @pl.loop(0, 8)
        def _(i):
            far = (y + i // 2 + jnp.where(khalf == c, 2, 0)) % 4
            j = far * 4 + zd * 2 + i % 2
            to = 16 * c + j
            src = og.at[pl.ds(pl.multiple_of(j * CS, CS), CS)]

            @pl.when(to != k)
            def _():
                remote(src, r_slot, r_send, r_recv, (d, to)).start()

            @pl.when(to == k)
            def _():
                pltpu.make_async_copy(src, r_slot, r_recv).start()

    def arrived(p):
        @pl.when(jnp.logical_or(p < d - 1, p > d + 1))
        def _():
            taken(sl.at[p + 1], s_recv.at[p])

    passed_on(send, arrived)

    def spread_chans(odd_plane, forward):
        @pl.loop(0, 8, unroll=2)
        def _(j):
            p = (j // 2) * NL + 2 * (j % 2) + odd_plane
            taken(v2.at[p], v_recv.at[p])
            if forward:
                remote(v2.at[p], v2.at[p], f_send, v_recv.at[p], (d, sib)).start()
            v = v2[p].astype(F32)
            xc[p, pl.ds(0, 64), :] = right(v).astype(BF16)
            xc[p, pl.ds(64, 64), :] = v2[p]
            xc[p, pl.ds(128, 64), :] = left(v).astype(BF16)

    spread_chans(c, True)

    spread_chans(1 - c, False)

    @pl.loop(0, ND)
    def _(p):
        @pl.when(p // NL != x)
        def _():
            arrived(p)

    @pl.loop(0, ND, unroll=4)
    def _(p):
        v = sl[p + 1].astype(F32)
        slb[p + 1, pl.ds(0, CS), :] = down(v).astype(BF16)
        slb[p + 1, pl.ds(CS, CS), :] = sl[p + 1]
        slb[p + 1, pl.ds(2 * CS, CS), :] = up(v).astype(BF16)

    for p in range(0, ND, 4):
        lhs = jnp.concatenate(
            [slb[pl.ds(p + i, 3)].reshape(9 * CS, VOX) for i in range(4)], axis=1
        )
        rhs = jnp.concatenate([xc[p + i] for i in range(4)], axis=1)
        part = lax.dot_general(lhs, rhs, (((1,), (1,)), ((), ())), preferred_element_type=F32)
        acc[...] = part if p == 0 else acc[...] + part

    for a in range(3):
        for b in range(3):
            rows = acc[pl.ds(((2 - a) * 3 + b) * CS, CS), :]
            for cc in range(3):
                part = rows[:, cc * 64 : cc * 64 + 64]
                kg_ref[a * 9 + b * 3 + cc] = part

    k_out.wait_send()
    for own, sem in ((self_a, a_send), (self_a, r_send)):
        @pl.when(own)
        def _():
            taken(xh.at[pl.ds(0, 15 * CS)], sem)

        @pl.when(jnp.logical_not(own))
        def _():
            taken(xh, sem)

    @pl.when(self_v)
    def _():
        taken(v2.at[pl.ds(0, 7)], v_send)

    @pl.when(jnp.logical_not(self_v))
    def _():
        taken(v2.at[pl.ds(0, 8)], v_send)

    taken(v2.at[pl.ds(0, 8)], f_send)
    taken(psend.at[1, 1], p_send.at[2])

    @pl.when(not_last)
    def _():
        for r in range(2):
            taken(psend.at[0, r], p_send.at[3 + r])
        taken(mine, n_send.at[2])

    @pl.when(not_first)
    def _():
        for r in range(2):
            taken(psend.at[2, r], p_send.at[5 + r])
        taken(mine, n_send.at[0])

    taken(mine, n_send.at[1])

    own_copies(sent)
    own_along(sent)
    passed_on(sent, lambda p: None)

    taken(rs, r_recv)
    total = rs[0].astype(F32)
    for j in range(1, 16):
        total = total + rs[j].astype(F32)
    ig_ref[...] = total.T.astype(BF16)


def local(volume, cotangent, kernel):
    in_hbm = pl.BlockSpec(memory_space=pltpu.HBM)
    in_vmem = pl.BlockSpec(memory_space=pltpu.VMEM)
    dma = pltpu.SemaphoreType.DMA
    ig, kg = pl.pallas_call(
        kernel_body,
        out_shape=(
            jax.ShapeDtypeStruct((VOX, CS), BF16),
            jax.ShapeDtypeStruct((TAPS, CS, 64), F32),
        ),
        in_specs=[in_hbm] * 3,
        out_specs=(in_vmem, in_vmem),
        scratch_shapes=[
            pltpu.VMEM((VOX, CS), BF16),
            pltpu.VMEM((VOX, CS), BF16),
            pltpu.VMEM((CS, VOX), BF16),
            pltpu.VMEM((HALF, VOX), BF16),
                    pltpu.VMEM((28, O2, HALF), BF16),
            pltpu.VMEM((HALF, TPAD), BF16),
            pltpu.VMEM((3, 2, CS, VOX), BF16),
            pltpu.VMEM((3, 2, CS, VOX), BF16),
            pltpu.VMEM((CS, VOX), F32),
            pltpu.VMEM((ND + 2, CS, VOX), BF16),
            pltpu.VMEM((3, CS, VOX), BF16),
            pltpu.VMEM((TPAD, VOX), BF16),
            pltpu.VMEM((HALF, VOX), BF16),
            pltpu.VMEM((16, CS, VOX), BF16),
            pltpu.VMEM((ND, 64, VOX), BF16),
            pltpu.VMEM((ND, 192, VOX), BF16),
            pltpu.VMEM((ND + 2, 3 * CS, VOX), BF16),
            pltpu.VMEM((9 * CS, 192), F32),
            dma((3,)), dma, dma, dma, dma((2,)), dma((7,)), dma((3, 2)), dma((32,)), dma((ND,)),
            dma((3,)), dma((3,)), dma, dma((ND,)), dma, dma, dma,
        ],
        compiler_params=pltpu.CompilerParams(
            collective_id=0, has_side_effects=True, vmem_limit_bytes=48 * 2**20
        ),
        cost_estimate=pl.CostEstimate(
            flops=3 * 453_000_000, bytes_accessed=6_000_000, transcendentals=8192
        ),
    )(
        pltpu.with_memory_space_constraint(volume.reshape(VOX, CS), pltpu.HBM),
        pltpu.with_memory_space_constraint(cotangent.reshape(VOX, CS), pltpu.HBM),
        pltpu.with_memory_space_constraint(jnp.transpose(kernel, (1, 0, 2)), pltpu.HBM),
    )
    ig, kg = pl.pallas_call(
        finish,
        out_shape=(
            jax.ShapeDtypeStruct((VOX, CS), BF16),
            jax.ShapeDtypeStruct((TAPS, CS, 64), F32),
        ),
        in_specs=[pl.BlockSpec(memory_space=pl.ANY)] * 2,
        out_specs=(pl.BlockSpec(memory_space=pl.ANY),) * 2,
        scratch_shapes=[dma((2,))],
    )(*(pltpu.with_memory_space_constraint(v, pltpu.VMEM) for v in (ig, kg)))
    input_grad = ig.reshape(1, SIDE, SIDE, CS)
    kernel_grad = jnp.transpose(kg, (1, 0, 2))[None]
    return (input_grad, kernel_grad)


def solution(mesh):
    return jax.shard_map(
        local,
        mesh=mesh,
        in_specs=(
            P("depth", None, None, "chan"),
            P("depth", None, None, "chan"),
            P("chan", None, None),
        ),
        out_specs=(P("depth", None, None, "chan"), P("chan", None, None, "depth")),
        check_vma=False,
    )
```
